256 devices in a mesh: inst: 32 (over y, z), tp: 8 (over x, core).
Axes of the slice: x: 4, y: 4, z: 8, core: 2. Of those that a mesh axis runs over, the one named last changes fastest.
Arguments:
- query: bfloat16 [256, 64, 128], P('inst', 'tp'), may hold values from -33 to 33
- new_key: bfloat16 [256, 8, 128], P('inst', 'tp'), may hold values from -6 to 6
- new_value: bfloat16 [256, 8, 128], P('inst', 'tp'), may hold values from -10 to 10
- key_cache: bfloat16 [1024, 256, 8, 128], P('inst', None, 'tp'), may hold values from -8 to 8
- value_cache: bfloat16 [1024, 256, 8, 128], P('inst', None, 'tp'), may hold values from -10 to 10
- out_weight: bfloat16 [8192, 4096], P('tp'), may hold values from -0.09375 to 0.09375
- lengths: int32 [256], replicated, may hold values from 1 to 4096, as said below
- block_owner: int32 [1024], P('inst'), may hold values from -1 to 255, as said below
- block_index: int32 [1024], P('inst'), may hold values from 0 to 15, as said below
Outputs:
- mixed: bfloat16 [256, 4096], P('inst', 'tp')
The draws below stay inside these ranges and needn't reach their ends.
Inputs may be any that keep to these rules, and one draw needn't show every extreme that they name: `lengths`: requests of instance i are rows i * 8 to i * 8 + 7. Some request holds exactly 4096 tokens and some holds 1. `block_owner`: A request of length L has exactly ceil(L / 256) blocks, each (request, block) pair in exactly one slot, on the request's own instance or on a lending instance; other slots hold -1. For any two different instances i and j, at most 4 slots of i hold blocks of requests of j, and exactly 4 for some pair. The slot holds tokens block_index * 256 to block_index * 256 + 255 of its request; 0 in free slots.
All inputs are finite; a program needn't handle non-finite values.
Results may differ from the reference program's by a relative error of at most 0.022.
Values may be sent and summed in bfloat16 or wider, within the bound.
No kernel may reach another device: no remote copies, remote signals or barrier semaphores. Data moves between devices by JAX's collectives and lax.ppermute only.
A program may use at most 64 MiB of HBM per device.

```python
import jax
import jax.numpy as jnp
from jax import lax

QH = 64
KVH = 8
HD = 128
DW = 4096
BLOCK = 256
MAXB = 16
REQ_INST = 8
POOL = 32
RG = 256
N_INST = 32


def layout_of(key):
    key = jax.random.fold_in(key, 202)
    key_order, key_heavy, key_light = jax.random.split(key, 3)
    slot_total = N_INST * POOL
    heavy_total = N_INST // 8
    lender_total = N_INST - heavy_total
    offset = jax.random.randint(key_order, (), 0, N_INST).astype(jnp.int32)
    all_ids = jnp.arange(N_INST, dtype=jnp.int32)
    relative = (all_ids - offset) % N_INST
    rel_ids = jnp.arange(N_INST, dtype=jnp.int32)
    half_way = N_INST // 2
    heavy_rel = (rel_ids % 2 == 0) & (rel_ids < 2 * heavy_total)
    first_rel = (rel_ids >= half_way) & ((rel_ids - half_way) % 2 == 0) & (rel_ids < half_way + 2 * heavy_total)
    other_rel = jnp.logical_not(heavy_rel | first_rel).astype(jnp.int32)
    other_rank = (jnp.cumsum(other_rel) - other_rel).astype(jnp.int32)
    rank_by_rel = jnp.where(heavy_rel, lender_total + rel_ids // 2, jnp.where(first_rel, (rel_ids - half_way) // 2, heavy_total + other_rank)).astype(jnp.int32)
    rank_of = rank_by_rel[relative]
    lender_order = jnp.zeros((N_INST,), jnp.int32).at[rank_of].set(all_ids)
    is_heavy = rank_of >= lender_total
    first_heavy = rank_of == lender_total
    longest = MAXB * BLOCK
    heavy_len = jax.random.randint(key_heavy, (N_INST, REQ_INST), MAXB // 2 * BLOCK + 1, longest + 1)
    light_len = jax.random.randint(key_light, (N_INST, REQ_INST), 1, MAXB // 8 * BLOCK + 1)
    column = jnp.arange(REQ_INST, dtype=jnp.int32)[None, :]
    heavy_len = jnp.where((column == 0) | first_heavy[:, None], longest, heavy_len)
    light_len = jnp.where(column == REQ_INST - 1, 1, light_len)
    context = jnp.where(is_heavy[:, None], heavy_len, light_len).astype(jnp.int32)
    block_counts = (context + BLOCK - 1) // BLOCK
    block_ids = jnp.arange(MAXB, dtype=jnp.int32)
    present = (block_ids[None, None, :] < block_counts[:, :, None]).reshape(N_INST, REQ_INST * MAXB).astype(jnp.int32)
    home_rank = (jnp.cumsum(present, axis=1) - present).astype(jnp.int32)
    at_home = (present == 1) & (home_rank < POOL)
    is_spill = (present == 1) & (home_rank >= POOL)
    present_total = jnp.sum(present, axis=1).astype(jnp.int32)
    used_count = jnp.minimum(present_total, POOL)
    spill_count = jnp.maximum(present_total - POOL, 0)
    heavy_ids = lender_order[lender_total:]
    heavy_spill = spill_count[heavy_ids]
    heavy_rows = jnp.arange(heavy_total, dtype=jnp.int32)[:, None]
    lender_cols = jnp.arange(lender_total, dtype=jnp.int32)[None, :]
    residue = (lender_cols - heavy_rows) % lender_total
    counts = jnp.maximum((heavy_spill[:, None] - residue + lender_total - 1) // lender_total, 0)
    before = (jnp.cumsum(counts, axis=0) - counts).astype(jnp.int32)
    heavy_rank = jnp.clip(rank_of - lender_total, 0, heavy_total - 1)
    spill_pos = jnp.maximum(home_rank - POOL, 0)
    lender_pick = (spill_pos + heavy_rank[:, None]) % lender_total
    lender_inst = lender_order[lender_pick]
    spill_target = lender_inst * POOL + used_count[lender_inst] + before[heavy_rank[:, None], lender_pick] + spill_pos // lender_total
    instance_ids = jnp.arange(N_INST, dtype=jnp.int32)[:, None]
    home_target = instance_ids * POOL + home_rank
    target = jnp.where(at_home, home_target, jnp.where(is_spill, spill_target, slot_total)).reshape(-1).astype(jnp.int32)
    request_ids = instance_ids * REQ_INST + jnp.arange(REQ_INST, dtype=jnp.int32)[None, :]
    request_of = jnp.broadcast_to(request_ids[:, :, None], (N_INST, REQ_INST, MAXB)).reshape(-1)
    position_of = jnp.broadcast_to(block_ids[None, None, :], (N_INST, REQ_INST, MAXB)).reshape(-1)
    owners = jnp.full((slot_total,), -1, jnp.int32).at[target].set(request_of, mode='drop')
    positions = jnp.zeros((slot_total,), jnp.int32).at[target].set(position_of, mode='drop')
    return (context.reshape(-1), owners, positions)


def draw_lengths(key, part):
    shared = layout_of(key)
    return shared[0]


def draw_block_owner(key, part):
    shared = layout_of(key)
    return shared[1]


def draw_block_index(key, part):
    shared = layout_of(key)
    return shared[2]


def draw_query(key, part):
    key = jax.random.fold_in(key, 6)
    key_one = jax.random.fold_in(key, 0)
    request_total = N_INST * REQ_INST
    values_out = jnp.clip(2.0 * jax.random.normal(key_one, (request_total, QH, HD), jnp.float32), -8.0, 8.0)
    return values_out.astype(jnp.bfloat16)


def draw_key_cache(key, part):
    key = jax.random.fold_in(key, 7)
    key_one = jax.random.fold_in(key, 0)
    shape_all = (N_INST * POOL, BLOCK, KVH, HD)
    values_out = jnp.clip(jax.random.normal(key_one, shape_all, jnp.float32), -6.0, 6.0)
    return values_out.astype(jnp.bfloat16)


def spiked(result, rng, source, target, parts, factor):
    def block_of(axis_at):
        return (jnp.arange(result.shape[axis_at]) // (result.shape[axis_at] // parts)).reshape((-1,) + (1,) * (result.ndim - 1 - axis_at))

    one_side = jax.random.permutation(rng, parts)[block_of(target)]
    far = (block_of(target) + parts // 2) % parts
    return jnp.where((block_of(source) == one_side) | (block_of(source) == far), factor * result, result)


def steps_of(own_key, shape, cuts, least, largest):
    level = 1.0
    for dim, shards_of in cuts:
        steps = jax.random.uniform(jax.random.fold_in(jax.random.fold_in(own_key, 6), dim), (shards_of,), jnp.float32, least / len(cuts), largest / len(cuts))
        level = level * jnp.repeat(jnp.exp(steps), shape[dim] // shards_of).reshape((-1,) + (1,) * (len(shape) - 1 - dim))
    return level


def normal_values(stream_key, shape, spread, limit, cuts=(), held_as=jnp.bfloat16):
    values = spread * jax.random.normal(stream_key, shape, jnp.float32)
    if cuts:
        values = values * steps_of(stream_key, shape, cuts, -0.22, 0.18)
    return jnp.clip(values, -limit, limit).astype(held_as)


def bell_draw_with(stream_key, shape, spread, most, shards, heavy, kind=jnp.bfloat16):
    entries = spread * jax.random.normal(stream_key, shape, jnp.float32)
    if shards:
        entries = entries * steps_of(stream_key, shape, shards, -0.22, 0.18)
    return jnp.clip(spiked(entries, jax.random.fold_in(stream_key, 3), *heavy), -most, most).astype(kind)


def setup_inputs(seed: int = 0) -> dict:
    key_of = jax.random.split(jax.random.key(seed), 10)
    query = draw_query(jax.random.fold_in(key_of[9], 71), 0)
    new_key = normal_values(key_of[1], (RG, KVH, HD), 1.0, 6.0, ((0, 32), (1, 8)))
    new_value = normal_values(key_of[2], (RG, KVH, HD), 2.0, 10.0, ((0, 32), (1, 8)))
    key_cache = draw_key_cache(jax.random.fold_in(key_of[9], 71), 0)
    value_cache = normal_values(key_of[4], (N_INST * POOL, BLOCK, KVH, HD), 2.0, 10.0, ((0, 32), (2, 8)))
    out_weight = bell_draw_with(key_of[5], (QH * HD, DW), (QH * HD) ** -0.5, 0.09375, ((0, 8),), (0, 1, 8, 2.0))
    lengths = draw_lengths(jax.random.fold_in(key_of[9], 71), 0)
    block_owner = draw_block_owner(jax.random.fold_in(key_of[9], 71), 0)
    block_index = draw_block_index(jax.random.fold_in(key_of[9], 71), 0)
    return {"query": query, "new_key": new_key, "new_value": new_value, "key_cache": key_cache, "value_cache": value_cache, "out_weight": out_weight, "lengths": lengths, "block_owner": block_owner, "block_index": block_index}


masked_score = -1e30


def reference(query, new_key, new_value, key_cache, value_cache, out_weight, lengths, block_owner, block_index):
    total_req, heads, head_dim = query.shape
    kv_heads = new_key.shape[1]
    per_kv = heads // kv_heads
    softmax_scale = head_dim ** -0.5
    slot_count = key_cache.shape[0] // N_INST
    block_len = key_cache.shape[1]
    grouped_query = query.astype(jnp.float32).reshape(total_req, kv_heads, per_kv, head_dim)
    keys_split = key_cache.reshape(N_INST, slot_count, block_len, kv_heads, head_dim)
    values_split = value_cache.reshape(N_INST, slot_count, block_len, kv_heads, head_dim)
    owners_split = block_owner.reshape(N_INST, slot_count)
    index_split = block_index.reshape(N_INST, slot_count)

    def block_scores(key_block, owner_ids, index_ids):
        holder = jnp.maximum(owner_ids, 0).astype(jnp.int32)
        picked = grouped_query[holder]
        scores = jnp.einsum("pkgd,ptkd->pkgt", picked, key_block.astype(jnp.float32)) * softmax_scale
        positions = index_ids[:, None] * block_len + jnp.arange(block_len, dtype=jnp.int32)[None, :]
        usable = (owner_ids >= 0)[:, None] & (positions < lengths[holder][:, None])
        usable = usable[:, None, None, :]
        return jnp.where(usable, scores, masked_score), holder, usable

    def find_max(current, block_args):
        key_block, owner_ids, index_ids = block_args
        scores, holder, usable = block_scores(key_block, owner_ids, index_ids)
        block_top = jnp.max(scores, axis=3)
        return current.at[holder].max(block_top), None

    start_max = jnp.full((total_req, kv_heads, per_kv), masked_score, jnp.float32)
    cache_max, _ = lax.scan(find_max, start_max, (keys_split, owners_split, index_split))
    own_scores = jnp.einsum("rkgd,rkd->rkg", grouped_query, new_key.astype(jnp.float32)) * softmax_scale
    row_max = jnp.maximum(cache_max, own_scores)

    def accumulate(current, block_args):
        running_sum, running_out = current
        key_block, value_block, owner_ids, index_ids = block_args
        scores, holder, usable = block_scores(key_block, owner_ids, index_ids)
        weights = jnp.where(usable, jnp.exp(scores - row_max[holder][..., None]), 0.0)
        weights = lax.optimization_barrier(weights.astype(jnp.bfloat16)).astype(jnp.float32)
        block_sum = jnp.sum(weights, axis=3)
        block_out = jnp.einsum("pkgt,ptkd->pkgd", weights, value_block.astype(jnp.float32))
        return (running_sum.at[holder].add(block_sum), running_out.at[holder].add(block_out)), None

    start_sum = jnp.zeros((total_req, kv_heads, per_kv), jnp.float32)
    start_out = jnp.zeros((total_req, kv_heads, per_kv, head_dim), jnp.float32)
    (cache_sum, cache_out), _ = lax.scan(accumulate, (start_sum, start_out), (keys_split, values_split, owners_split, index_split))
    own_weight = lax.optimization_barrier(jnp.exp(own_scores - row_max).astype(jnp.bfloat16)).astype(jnp.float32)
    total = cache_sum + own_weight
    summed = cache_out + own_weight[..., None] * new_value.astype(jnp.float32)[:, :, None, :]
    attended = (summed / total[..., None]).astype(jnp.bfloat16).reshape(total_req, heads * head_dim)
    return jnp.dot(attended, out_weight, preferred_element_type=jnp.float32).astype(jnp.bfloat16)
```

```python
import jax
import jax.numpy as jnp
from jax import lax
from jax.experimental import pallas as pl
from jax.experimental.pallas import tpu as pltpu
from jax.sharding import PartitionSpec as P

masked_score = -1e30
lent_slots = 4
f32 = jnp.float32
bf16 = jnp.bfloat16


def attend_kernel(
    owner_ref, index_ref, length_ref, query_ref, key_ref, value_ref,
    sent_ref, local_out_ref, local_note_ref, entry_out, entry_note, used_count,
):
    slots, block_len, head_dim = key_ref.shape
    heads = 8
    n_inst = query_ref.shape[0] // (8 * heads)
    spare = n_inst * lent_slots
    scale = head_dim ** (-0.5)
    me = lax.axis_index("inst")
    token = lax.broadcasted_iota(jnp.int32, (heads, block_len), 1)
    lane = lax.broadcasted_iota(jnp.int32, (heads, head_dim), 1)
    kind = lane % 4
    group = lane // 4
    blank = jnp.where(kind == 3, -1.0, 0.0).astype(f32)

    for e in range(spare):
        entry_out[e] = jnp.zeros((heads, head_dim), f32)
        entry_note[e] = blank
    for j in range(n_inst):
        used_count[j] = 0

    owners = [owner_ref[p] for p in range(slots)]
    holders = [jnp.maximum(o, 0) for o in owners]
    scores = []
    for p in range(slots):
        pair = query_ref[pl.ds(pl.multiple_of((holders[p] // 2) * 16, 16), 16), :]
        both = lax.dot_general(
            pair, key_ref[p], (((1,), (1,)), ((), ())), preferred_element_type=f32
        )
        scores.append(jnp.where(holders[p] % 2 == 1, both[heads:], both[:heads]) * scale)
    notes = []
    for p in range(slots):
        limit = jnp.where(
            owners[p] >= 0, length_ref[holders[p]] - index_ref[p] * block_len, 0
        )
        live = token < limit
        score = jnp.where(live, scores[p], masked_score)
        top = jnp.max(score, axis=1, keepdims=True)
        top = (top + jnp.abs(top) * 0.0078125).astype(bf16).astype(f32)
        weight = jnp.where(live, jnp.exp(score - top), 0.0).astype(bf16)
        total = jnp.sum(weight.astype(f32), axis=1, keepdims=True)
        out = jnp.dot(weight, value_ref[p], preferred_element_type=f32)
        home = holders[p] // 8
        request = (holders[p] % 8).astype(f32)
        foreign = (owners[p] >= 0) & (home != me)
        local = (owners[p] >= 0) & (home == me)
        rank = used_count[home]
        used_count[home] = rank + foreign.astype(jnp.int32)
        place = jnp.where(foreign, home * lent_slots + rank, spare)
        high = total.astype(bf16).astype(f32)
        note = jnp.where(kind == 0, top, jnp.where(kind == 1, high, total - high))
        entry_out[place] = out
        entry_note[place] = jnp.where(kind == 3, request, note)
        local_out_ref[p] = out
        notes.append(jnp.where(kind == 3, jnp.where(local, request, -1.0), note))
        if p % 4 == 3:
            a, b, c, d = notes[p - 3 : p + 1]
            local_note_ref[p // 4] = jnp.where(
                group == 0, a, jnp.where(group == 1, b, jnp.where(group == 2, c, d))
            )
    for jj in range(n_inst // 2):
        rows = []
        for j in (2 * jj, 2 * jj + 1):
            a, b, c, d = [entry_note[j * lent_slots + k] for k in range(lent_slots)]
            rows += [entry_out[j * lent_slots + k] for k in range(lent_slots)]
            rows.append(
                jnp.where(group == 0, a, jnp.where(group == 1, b, jnp.where(group == 2, c, d)))
            )
        sent_ref[pl.ds(80 * jj, 80), :] = jnp.concatenate(rows, axis=0).astype(bf16)


def merge_kernel(
    got_ref, local_out_ref, local_note_ref, query_ref, new_key_ref, new_value_ref, weight_ref,
    attended_ref, send_ref, attended_rows,
):
    requests = 8
    heads = 8
    head_dim = query_ref.shape[1]
    scale = head_dim ** (-0.5)
    groups = got_ref.shape[0] // 40 + local_note_ref.shape[0]
    outs, notes = [], []
    for jj in range(got_ref.shape[0] // 80):
        block = got_ref[pl.ds(80 * jj, 80), :].astype(f32)
        for j in range(2):
            rows = block[40 * j : 40 * (j + 1)]
            outs.append([rows[8 * k : 8 * k + 8] for k in range(lent_slots)])
            notes.append(rows[32:40])
    for g in range(local_note_ref.shape[0]):
        outs.append([local_out_ref[4 * g + k] for k in range(lent_slots)])
        notes.append(local_note_ref[g])
    note = jnp.concatenate(notes, axis=0)
    lane = lax.broadcasted_iota(jnp.int32, note.shape, 1)
    holds = (lane % 4 == 0) & (lane < 4 * lent_slots)
    sums = pltpu.roll(note, head_dim - 1, 1) + pltpu.roll(note, head_dim - 2, 1)
    who = jnp.where(holds, pltpu.roll(note, head_dim - 3, 1), -1.0)
    shape = (groups, heads, head_dim)
    note, sums, who = note.reshape(shape), sums.reshape(shape), who.reshape(shape)

    query = query_ref[...].astype(f32).reshape(requests, heads, head_dim)
    new_key = new_key_ref[...].astype(f32)
    new_value = new_value_ref[...].astype(f32)
    tops, own_scores = [], []
    chosen = jnp.zeros(shape, f32)
    for r in range(requests):
        own = jnp.sum(query[r] * new_key[r : r + 1], axis=1, keepdims=True) * scale
        mine = jnp.max(jnp.where(who == r, note, masked_score), axis=0)
        top = jnp.maximum(jnp.max(mine, axis=1, keepdims=True), own)
        chosen = jnp.where(who == r, top[None], chosen)
        tops.append(top)
        own_scores.append(own)
    factor = jnp.where(who >= 0, jnp.exp(note - chosen), 0.0)
    scaled = factor * sums
    totals, values = [], []
    for r in range(requests):
        own_weight = jnp.exp(own_scores[r] - tops[r]).astype(bf16).astype(f32)
        cached = jnp.sum(jnp.where(who == r, scaled, 0.0), axis=0)
        totals.append(jnp.sum(cached, axis=1, keepdims=True) + own_weight)
        values.append(own_weight * new_value[r : r + 1])
    for g in range(groups):
        for k in range(lent_slots):
            at = slice(4 * k, 4 * k + 1)
            part = factor[g][:, at] * outs[g][k]
            whose = jnp.broadcast_to(who[g][:, at], part.shape)
            for r in range(requests):
                values[r] = values[r] + jnp.where(whose == r, part, 0.0)
    for r in range(requests):
        attended_rows[r] = values[r] / totals[r]
    attended = jnp.concatenate([attended_rows[:, h, :] for h in range(heads)], axis=1).astype(bf16)
    attended_ref[...] = attended
    other = 1 - lax.axis_index("tp") % 2
    width = send_ref.shape[1] // 4
    for n in range(4):
        at = pl.ds(pl.multiple_of((2 * n + other) * width, width), width)
        send_ref[:, n * width : (n + 1) * width] = jnp.dot(
            attended, weight_ref[:, at], preferred_element_type=f32
        ).astype(bf16)


def project_kernel(attended_ref, weight_ref, keep_ref):
    mine = lax.axis_index("tp") % 2
    width = keep_ref.shape[1] // 4
    attended = attended_ref[...]
    for n in range(4):
        at = pl.ds(pl.multiple_of((2 * n + mine) * width, width), width)
        keep_ref[:, n * width : (n + 1) * width] = jnp.dot(
            attended, weight_ref[:, at], preferred_element_type=f32
        )


def split_kernel(keep_ref, got_ref, own_ref, *send_refs):
    chip = lax.axis_index("tp") // 2
    width = own_ref.shape[1]
    for k in range(4):
        at = pl.ds(pl.multiple_of(lax.rem(chip + k, 4) * width, width), width)
        total = keep_ref[:, at] + got_ref[:, at].astype(f32)
        if k == 0:
            own_ref[...] = total
        else:
            send_refs[k - 1][...] = total.astype(bf16)


def vmem(n):
    return [pl.BlockSpec(memory_space=pltpu.VMEM)] * n


def smem(n):
    return [pl.BlockSpec(memory_space=pltpu.SMEM)] * n


def body(
    query, new_key, new_value, key_cache, value_cache, out_weight, lengths, block_owner, block_index
):
    req_local, heads_dev, head_dim = query.shape
    slot_count, block_len, _, _ = key_cache.shape
    n_inst = lengths.shape[0] // req_local
    n_tp = lax.axis_size("tp")
    rows = req_local * heads_dev
    features = out_weight.shape[1]
    params = pltpu.CompilerParams(vmem_limit_bytes=40 * 1024 * 1024)
    shape = jax.ShapeDtypeStruct

    flat_query = query.reshape(rows, head_dim)
    copies = jnp.broadcast_to(flat_query[None], (n_inst, rows, head_dim))
    everyone = lax.all_to_all(copies, "inst", 0, 0, tiled=True)
    keys = key_cache.reshape(slot_count, block_len, head_dim)
    values = value_cache.reshape(slot_count, block_len, head_dim)
    sent_rows = (lent_slots + 1) * heads_dev
    sent, local_out, local_note = pl.pallas_call(
        attend_kernel,
        out_shape=(
            shape((n_inst * sent_rows, head_dim), bf16),
            shape((slot_count, heads_dev, head_dim), f32),
            shape((slot_count // lent_slots, heads_dev, head_dim), f32),
        ),
        in_specs=smem(3) + vmem(3),
        out_specs=tuple(vmem(3)),
        scratch_shapes=[
            pltpu.VMEM((n_inst * lent_slots + 1, heads_dev, head_dim), f32),
            pltpu.VMEM((n_inst * lent_slots + 1, heads_dev, head_dim), f32),
            pltpu.SMEM((n_inst,), jnp.int32),
        ],
        compiler_params=params,
        name="attend",
    )(block_owner, block_index, lengths, everyone.reshape(n_inst * rows, head_dim), keys, values)
    got = lax.all_to_all(
        sent.reshape(n_inst, sent_rows, head_dim), "inst", 0, 0, tiled=True
    ).reshape(n_inst * sent_rows, head_dim)
    attended, for_core = pl.pallas_call(
        merge_kernel,
        out_shape=(
            shape((req_local, heads_dev * head_dim), bf16),
            shape((req_local, features // 2), bf16),
        ),
        in_specs=vmem(7),
        out_specs=tuple(vmem(2)),
        scratch_shapes=[pltpu.VMEM((req_local, heads_dev, head_dim), f32)],
        compiler_params=params,
        name="merge",
    )(
        got, local_out, local_note, flat_query,
        new_key.reshape(req_local, head_dim), new_value.reshape(req_local, head_dim), out_weight,
    )
    from_core = lax.ppermute(for_core, "tp", [(i, i ^ 1) for i in range(n_tp)])
    keep = pl.pallas_call(
        project_kernel,
        out_shape=shape((req_local, features // 2), f32),
        in_specs=vmem(2),
        out_specs=vmem(1)[0],
        compiler_params=params,
        cost_estimate=pl.CostEstimate(
            flops=req_local * heads_dev * head_dim * features, bytes_accessed=4194304, transcendentals=0
        ),
        name="project",
    )(attended, out_weight)
    width = features // n_tp
    own, *parts = pl.pallas_call(
        split_kernel,
        out_shape=(shape((req_local, width), f32),) + (shape((req_local, width), bf16),) * 3,
        in_specs=vmem(2),
        out_specs=tuple(vmem(4)),
        compiler_params=params,
        name="split",
    )(keep, from_core)
    total = own
    for k in (1, 2, 3):
        pairs = [(i, (i + 2 * k) % n_tp) for i in range(n_tp)]
        total = total + lax.ppermute(parts[k - 1], "tp", pairs).astype(f32)
    return total.astype(bf16)


def solution(mesh):
    placed = (
        P("inst", "tp", None),
        P("inst", "tp", None),
        P("inst", "tp", None),
        P("inst", None, "tp", None),
        P("inst", None, "tp", None),
        P("tp", None),
        P(),
        P("inst"),
        P("inst"),
    )
    return jax.shard_map(
        body, mesh=mesh, in_specs=placed, out_specs=P("inst", "tp"), check_vma=False
    )
```

```python
import jax
import jax.numpy as jnp
from jax import lax
from jax.experimental import pallas as pl
from jax.experimental.pallas import tpu as pltpu
from jax.sharding import PartitionSpec as P

masked_score = -1e30
lent_slots = 4
f32 = jnp.float32
bf16 = jnp.bfloat16


def copies_kernel(query_ref, copies_ref):
    for j in range(copies_ref.shape[0]):
        copies_ref[j] = query_ref[...]


def attend_kernel(
    owner_ref, index_ref, length_ref, query_ref, key_ref, value_ref,
    sent_ref, local_out_ref, local_note_ref, entry_out, entry_note, used_count,
):
    slots, block_len, head_dim = key_ref.shape
    heads = 8
    n_inst = query_ref.shape[0] // (8 * heads)
    spare = n_inst * lent_slots
    scale = head_dim ** (-0.5)
    me = lax.axis_index("inst")
    token = lax.broadcasted_iota(jnp.int32, (heads, block_len), 1)
    lane = lax.broadcasted_iota(jnp.int32, (heads, head_dim), 1)
    kind = lane % 4
    group = lane // 4
    blank = jnp.where(kind == 3, -1.0, 0.0).astype(f32)

    for e in range(spare):
        entry_out[e] = jnp.zeros((heads, head_dim), f32)
        entry_note[e] = blank
    for j in range(n_inst):
        used_count[j] = 0

    owners = [owner_ref[p] for p in range(slots)]
    holders = [jnp.maximum(o, 0) for o in owners]
    scores = []
    for p in range(slots):
        pair = query_ref[pl.ds(pl.multiple_of((holders[p] // 2) * 16, 16), 16), :]
        both = lax.dot_general(
            pair, key_ref[p], (((1,), (1,)), ((), ())), preferred_element_type=f32
        )
        scores.append(jnp.where(holders[p] % 2 == 1, both[heads:], both[:heads]) * scale)
    notes = []
    for p in range(slots):
        limit = jnp.where(
            owners[p] >= 0, length_ref[holders[p]] - index_ref[p] * block_len, 0
        )
        live = token < limit
        score = jnp.where(live, scores[p], masked_score)
        top = jnp.max(score, axis=1, keepdims=True)
        top = (top + jnp.abs(top) * 0.0078125).astype(bf16).astype(f32)
        weight = jnp.where(live, jnp.exp(score - top), 0.0).astype(bf16)
        total = jnp.sum(weight.astype(f32), axis=1, keepdims=True)
        out = jnp.dot(weight, value_ref[p], preferred_element_type=f32)
        home = holders[p] // 8
        request = (holders[p] % 8).astype(f32)
        foreign = (owners[p] >= 0) & (home != me)
        local = (owners[p] >= 0) & (home == me)
        rank = used_count[home]
        used_count[home] = rank + foreign.astype(jnp.int32)
        place = jnp.where(foreign, home * lent_slots + rank, spare)
        high = total.astype(bf16).astype(f32)
        note = jnp.where(kind == 0, top, jnp.where(kind == 1, high, total - high))
        entry_out[place] = out
        entry_note[place] = jnp.where(kind == 3, request, note)
        local_out_ref[p] = out
        notes.append(jnp.where(kind == 3, jnp.where(local, request, -1.0), note))
        if p % 4 == 3:
            a, b, c, d = notes[p - 3 : p + 1]
            local_note_ref[p // 4] = jnp.where(
                group == 0, a, jnp.where(group == 1, b, jnp.where(group == 2, c, d))
            )
    for jj in range(n_inst // 2):
        rows = []
        for j in (2 * jj, 2 * jj + 1):
            a, b, c, d = [entry_note[j * lent_slots + k] for k in range(lent_slots)]
            rows += [entry_out[j * lent_slots + k] for k in range(lent_slots)]
            rows.append(
                jnp.where(group == 0, a, jnp.where(group == 1, b, jnp.where(group == 2, c, d)))
            )
        sent_ref[pl.ds(80 * jj, 80), :] = jnp.concatenate(rows, axis=0).astype(bf16)


def merge_kernel(
    got_ref, local_out_ref, local_note_ref, query_ref, new_key_ref, new_value_ref, weight_ref,
    send_ref, keep_ref, attended_rows,
):
    requests = 8
    heads = 8
    head_dim = query_ref.shape[1]
    scale = head_dim ** (-0.5)
    groups = got_ref.shape[0] // 40 + local_note_ref.shape[0]
    outs, notes = [], []
    for jj in range(got_ref.shape[0] // 80):
        block = got_ref[pl.ds(80 * jj, 80), :].astype(f32)
        for j in range(2):
            rows = block[40 * j : 40 * (j + 1)]
            outs.append([rows[8 * k : 8 * k + 8] for k in range(lent_slots)])
            notes.append(rows[32:40])
    for g in range(local_note_ref.shape[0]):
        outs.append([local_out_ref[4 * g + k] for k in range(lent_slots)])
        notes.append(local_note_ref[g])
    note = jnp.concatenate(notes, axis=0)
    lane = lax.broadcasted_iota(jnp.int32, note.shape, 1)
    holds = (lane % 4 == 0) & (lane < 4 * lent_slots)
    sums = pltpu.roll(note, head_dim - 1, 1) + pltpu.roll(note, head_dim - 2, 1)
    who = jnp.where(holds, pltpu.roll(note, head_dim - 3, 1), -1.0)
    shape = (groups, heads, head_dim)
    note, sums, who = note.reshape(shape), sums.reshape(shape), who.reshape(shape)

    query = query_ref[...].astype(f32).reshape(requests, heads, head_dim)
    new_key = new_key_ref[...].astype(f32)
    new_value = new_value_ref[...].astype(f32)
    tops, own_scores = [], []
    chosen = jnp.zeros(shape, f32)
    for r in range(requests):
        own = jnp.sum(query[r] * new_key[r : r + 1], axis=1, keepdims=True) * scale
        mine = jnp.max(jnp.where(who == r, note, masked_score), axis=0)
        top = jnp.maximum(jnp.max(mine, axis=1, keepdims=True), own)
        chosen = jnp.where(who == r, top[None], chosen)
        tops.append(top)
        own_scores.append(own)
    factor = jnp.where(who >= 0, jnp.exp(note - chosen), 0.0)
    scaled = factor * sums
    totals, values = [], []
    for r in range(requests):
        own_weight = jnp.exp(own_scores[r] - tops[r]).astype(bf16).astype(f32)
        cached = jnp.sum(jnp.where(who == r, scaled, 0.0), axis=0)
        totals.append(jnp.sum(cached, axis=1, keepdims=True) + own_weight)
        values.append(own_weight * new_value[r : r + 1])
    for g in range(groups):
        for k in range(lent_slots):
            at = slice(4 * k, 4 * k + 1)
            part = factor[g][:, at] * outs[g][k]
            whose = jnp.broadcast_to(who[g][:, at], part.shape)
            for r in range(requests):
                values[r] = values[r] + jnp.where(whose == r, part, 0.0)
    for r in range(requests):
        attended_rows[r] = values[r] / totals[r]
    attended = jnp.concatenate([attended_rows[:, h, :] for h in range(heads)], axis=1).astype(bf16)
    other = 1 - lax.axis_index("tp") % 2
    width = send_ref.shape[1] // 4
    for n in range(4):
        at = pl.ds(pl.multiple_of((2 * n + other) * width, width), width)
        send_ref[:, n * width : (n + 1) * width] = jnp.dot(
            attended, weight_ref[:, at], preferred_element_type=f32
        ).astype(bf16)
        at = pl.ds(pl.multiple_of((2 * n + 1 - other) * width, width), width)
        keep_ref[:, n * width : (n + 1) * width] = jnp.dot(
            attended, weight_ref[:, at], preferred_element_type=f32
        )


def split_kernel(keep_ref, got_ref, own_ref, *send_refs):
    chip = lax.axis_index("tp") // 2
    width = own_ref.shape[1]
    for k in range(4):
        at = pl.ds(pl.multiple_of(lax.rem(chip + k, 4) * width, width), width)
        total = keep_ref[:, at] + got_ref[:, at].astype(f32)
        if k == 0:
            own_ref[...] = total
        else:
            send_refs[k - 1][...] = total.astype(bf16)


def vmem(n):
    return [pl.BlockSpec(memory_space=pltpu.VMEM)] * n


def smem(n):
    return [pl.BlockSpec(memory_space=pltpu.SMEM)] * n


def body(
    query, new_key, new_value, key_cache, value_cache, out_weight, lengths, block_owner, block_index
):
    req_local, heads_dev, head_dim = query.shape
    slot_count, block_len, _, _ = key_cache.shape
    n_inst = lengths.shape[0] // req_local
    n_tp = lax.axis_size("tp")
    rows = req_local * heads_dev
    features = out_weight.shape[1]
    params = pltpu.CompilerParams(vmem_limit_bytes=24 * 1024 * 1024)
    shape = jax.ShapeDtypeStruct

    flat_query = query.reshape(rows, head_dim)
    copies = pl.pallas_call(
        copies_kernel,
        out_shape=shape((n_inst, rows, head_dim), bf16),
        in_specs=vmem(1),
        out_specs=vmem(1)[0],
        compiler_params=params,
        cost_estimate=pl.CostEstimate(flops=20_000_000_000, bytes_accessed=1_000_000, transcendentals=0),
        name="copies",
    )(flat_query)
    everyone = lax.all_to_all(copies, "inst", 0, 0, tiled=True)
    keys = key_cache.reshape(slot_count, block_len, head_dim)
    values = value_cache.reshape(slot_count, block_len, head_dim)
    sent_rows = (lent_slots + 1) * heads_dev
    sent, local_out, local_note = pl.pallas_call(
        attend_kernel,
        out_shape=(
            shape((n_inst * sent_rows, head_dim), bf16),
            shape((slot_count, heads_dev, head_dim), f32),
            shape((slot_count // lent_slots, heads_dev, head_dim), f32),
        ),
        in_specs=smem(3) + vmem(3),
        out_specs=tuple(vmem(3)),
        scratch_shapes=[
            pltpu.VMEM((n_inst * lent_slots + 1, heads_dev, head_dim), f32),
            pltpu.VMEM((n_inst * lent_slots + 1, heads_dev, head_dim), f32),
            pltpu.SMEM((n_inst,), jnp.int32),
        ],
        compiler_params=params,
        name="attend",
    )(block_owner, block_index, lengths, everyone.reshape(n_inst * rows, head_dim), keys, values)
    got = lax.all_to_all(
        sent.reshape(n_inst, sent_rows, head_dim), "inst", 0, 0, tiled=True
    ).reshape(n_inst * sent_rows, head_dim)
    for_core, keep = pl.pallas_call(
        merge_kernel,
        out_shape=(
            shape((req_local, features // 2), bf16),
            shape((req_local, features // 2), f32),
        ),
        in_specs=vmem(7),
        out_specs=tuple(vmem(2)),
        scratch_shapes=[pltpu.VMEM((req_local, heads_dev, head_dim), f32)],
        compiler_params=params,
        name="merge",
    )(
        got, local_out, local_note, flat_query,
        new_key.reshape(req_local, head_dim), new_value.reshape(req_local, head_dim), out_weight,
    )
    from_core = lax.ppermute(for_core, "tp", [(i, i ^ 1) for i in range(n_tp)])
    width = features // n_tp
    own, *parts = pl.pallas_call(
        split_kernel,
        out_shape=(shape((req_local, width), f32),) + (shape((req_local, width), bf16),) * 3,
        in_specs=vmem(2),
        out_specs=tuple(vmem(4)),
        compiler_params=params,
        name="split",
    )(keep, from_core)
    total = own
    for k in (1, 2, 3):
        pairs = [(i, (i + 2 * k) % n_tp) for i in range(n_tp)]
        total = total + lax.ppermute(parts[k - 1], "tp", pairs).astype(f32)
    return total.astype(bf16)


def solution(mesh):
    placed = (
        P("inst", "tp", None),
        P("inst", "tp", None),
        P("inst", "tp", None),
        P("inst", None, "tp", None),
        P("inst", None, "tp", None),
        P("tp", None),
        P(),
        P("inst"),
        P("inst"),
    )
    return jax.shard_map(
        body, mesh=mesh, in_specs=placed, out_specs=P("inst", "tp"), check_vma=False
    )
```

```python
import jax
import jax.numpy as jnp
from jax import lax
from jax.experimental import pallas as pl
from jax.experimental.pallas import tpu as pltpu
from jax.sharding import Mesh
from jax.sharding import PartitionSpec as P

masked_score = -1e30
lent_slots = 4
inst = ("y", "z")
ring_y = 4
f32 = jnp.float32
bf16 = jnp.bfloat16


def copies_kernel(query_ref, copies_ref):
    for j in range(copies_ref.shape[0]):
        copies_ref[j] = query_ref[...]


def attend_kernel(
    owner_ref, index_ref, length_ref, row0_ref, row1_ref, row2_ref, row3_ref, key_ref, value_ref,
    sent_ref, local_out_ref, local_note_ref, entry_out, entry_note, used_count,
):
    slots, block_len, head_dim = key_ref.shape
    heads = 8
    row_refs = (row0_ref, row1_ref, row2_ref, row3_ref)
    row_requests = row0_ref.shape[0] // heads
    n_inst = ring_y * row_requests // 8
    spare = n_inst * lent_slots
    scale = head_dim ** (-0.5)
    my_row = lax.axis_index("y")
    me = lax.axis_index(inst)
    token = lax.broadcasted_iota(jnp.int32, (heads, block_len), 1)
    lane = lax.broadcasted_iota(jnp.int32, (heads, head_dim), 1)
    kind = lane % 4
    group = lane // 4
    blank = jnp.where(kind == 3, -1.0, 0.0).astype(f32)

    for e in range(spare):
        entry_out[e] = jnp.zeros((heads, head_dim), f32)
        entry_note[e] = blank
    for j in range(n_inst):
        used_count[j] = 0

    owners = [owner_ref[p] for p in range(slots)]
    holders = [jnp.maximum(o, 0) for o in owners]
    scores = []
    for p in range(slots):
        back = lax.rem(my_row + ring_y - holders[p] // row_requests, ring_y)
        at = pl.ds(pl.multiple_of((lax.rem(holders[p], row_requests) // 2) * 16, 16), 16)
        pair = row_refs[0][at, :]
        for k in range(1, ring_y):
            pair = jnp.where(back == k, row_refs[k][at, :], pair)
        both = lax.dot_general(
            pair, key_ref[p], (((1,), (1,)), ((), ())), preferred_element_type=f32
        )
        scores.append(jnp.where(holders[p] % 2 == 1, both[heads:], both[:heads]) * scale)
    notes = []
    for p in range(slots):
        limit = jnp.where(
            owners[p] >= 0, length_ref[holders[p]] - index_ref[p] * block_len, 0
        )
        live = token < limit
        score = jnp.where(live, scores[p], masked_score)
        top = jnp.max(score, axis=1, keepdims=True)
        top = (top + jnp.abs(top) * 0.0078125).astype(bf16).astype(f32)
        weight = jnp.where(live, jnp.exp(score - top), 0.0).astype(bf16)
        total = jnp.sum(weight.astype(f32), axis=1, keepdims=True)
        out = jnp.dot(weight, value_ref[p], preferred_element_type=f32)
        home = holders[p] // 8
        request = (holders[p] % 8).astype(f32)
        foreign = (owners[p] >= 0) & (home != me)
        local = (owners[p] >= 0) & (home == me)
        rank = used_count[home]
        used_count[home] = rank + foreign.astype(jnp.int32)
        place = jnp.where(foreign, home * lent_slots + rank, spare)
        high = total.astype(bf16).astype(f32)
        note = jnp.where(kind == 0, top, jnp.where(kind == 1, high, total - high))
        entry_out[place] = out
        entry_note[place] = jnp.where(kind == 3, request, note)
        local_out_ref[p] = out
        notes.append(jnp.where(kind == 3, jnp.where(local, request, -1.0), note))
        if p % 4 == 3:
            a, b, c, d = notes[p - 3 : p + 1]
            local_note_ref[p // 4] = jnp.where(
                group == 0, a, jnp.where(group == 1, b, jnp.where(group == 2, c, d))
            )
    for jj in range(n_inst // 2):
        rows = []
        for j in (2 * jj, 2 * jj + 1):
            a, b, c, d = [entry_note[j * lent_slots + k] for k in range(lent_slots)]
            rows += [entry_out[j * lent_slots + k] for k in range(lent_slots)]
            rows.append(
                jnp.where(group == 0, a, jnp.where(group == 1, b, jnp.where(group == 2, c, d)))
            )
        sent_ref[pl.ds(80 * jj, 80), :] = jnp.concatenate(rows, axis=0).astype(bf16)


def merge_kernel(
    got_ref, local_out_ref, local_note_ref, query_ref, new_key_ref, new_value_ref, weight_ref,
    attended_ref, send_ref, attended_rows,
):
    heads = 8
    rows, head_dim = query_ref.shape
    requests = rows // heads
    scale = head_dim ** (-0.5)
    outs, notes = [], []
    for jj in range(got_ref.shape[0] // 80):
        block = got_ref[pl.ds(80 * jj, 80), :].astype(f32)
        for start in (0, 40):
            outs.append([block[start + 8 * k : start + 8 * k + 8] for k in range(lent_slots)])
            notes.append(block[start + 32 : start + 40])
    for g in range(local_note_ref.shape[0]):
        outs.append([local_out_ref[4 * g + k] for k in range(lent_slots)])
        notes.append(local_note_ref[g])
    while len(notes) % 16:
        outs.append([jnp.zeros((heads, head_dim), f32)] * lent_slots)
        notes.append(jnp.full((heads, head_dim), -1.0, f32))
    turned = jnp.concatenate(
        [jnp.concatenate(notes[g : g + 16], axis=0).T[:16] for g in range(0, len(notes), 16)], axis=1
    )
    entries = turned.shape[1]
    head_of = lax.broadcasted_iota(jnp.int32, (1, entries), 1) % heads
    row_id = lax.broadcasted_iota(jnp.int32, (rows, entries), 0).astype(f32)

    spread = (requests, heads, head_dim)
    new_key = jnp.broadcast_to(new_key_ref[...].astype(f32)[:, None, :], spread).reshape(rows, head_dim)
    new_value = jnp.broadcast_to(new_value_ref[...].astype(f32)[:, None, :], spread).reshape(rows, head_dim)
    own = jnp.sum(query_ref[...].astype(f32) * new_key, axis=1, keepdims=True) * scale

    tops = []
    for k in range(lent_slots):
        whose = turned[4 * k + 3 : 4 * k + 4] * heads + head_of.astype(f32)
        tops.append(jnp.where(row_id == whose, turned[4 * k : 4 * k + 1], masked_score))
    most = jnp.maximum(jnp.maximum(tops[0], tops[1]), jnp.maximum(tops[2], tops[3]))
    top = jnp.maximum(jnp.max(most, axis=1, keepdims=True), own)
    own_weight = jnp.exp(own - top).astype(bf16).astype(f32)
    total = 0.0
    value = own_weight * new_value
    for k in range(lent_slots):
        factor = jnp.exp(tops[k] - top).astype(bf16)
        sums = turned[4 * k + 1 : 4 * k + 2] + turned[4 * k + 2 : 4 * k + 3]
        total = total + factor.astype(f32) * sums
        part = jnp.concatenate([out[k] for out in outs], axis=0).astype(bf16)
        value = value + jnp.dot(factor, part, preferred_element_type=f32)
    total = jnp.sum(total, axis=1, keepdims=True) + own_weight
    attended_rows[...] = (value / total).reshape(spread)
    attended = jnp.concatenate([attended_rows[:, h, :] for h in range(heads)], axis=1).astype(bf16)
    attended_ref[...] = attended
    other = 1 - lax.axis_index("tp") % 2
    width = send_ref.shape[1] // 4
    for n in range(4):
        at = pl.ds(pl.multiple_of((2 * n + other) * width, width), width)
        send_ref[:, n * width : (n + 1) * width] = jnp.dot(
            attended, weight_ref[:, at], preferred_element_type=f32
        ).astype(bf16)


def project_kernel(attended_ref, weight_ref, keep_ref):
    mine = lax.axis_index("tp") % 2
    width = keep_ref.shape[1] // 4
    attended = attended_ref[...]
    for n in range(4):
        at = pl.ds(pl.multiple_of((2 * n + mine) * width, width), width)
        keep_ref[:, n * width : (n + 1) * width] = jnp.dot(
            attended, weight_ref[:, at], preferred_element_type=f32
        )


def split_kernel(keep_ref, got_ref, own_ref, *send_refs):
    chip = lax.axis_index("tp") // 2
    width = own_ref.shape[1]
    for k in range(4):
        at = pl.ds(pl.multiple_of(lax.rem(chip + k, 4) * width, width), width)
        total = keep_ref[:, at] + got_ref[:, at].astype(f32)
        if k == 0:
            own_ref[...] = total
        else:
            send_refs[k - 1][...] = total.astype(bf16)


def vmem(n):
    return [pl.BlockSpec(memory_space=pltpu.VMEM)] * n


def smem(n):
    return [pl.BlockSpec(memory_space=pltpu.SMEM)] * n


def body(
    query, new_key, new_value, key_cache, value_cache, out_weight, lengths, block_owner, block_index
):
    req_local, heads_dev, head_dim = query.shape
    slot_count, block_len, _, _ = key_cache.shape
    n_inst = lengths.shape[0] // req_local
    ring_z = n_inst // ring_y
    n_tp = lax.axis_size("tp")
    rows = req_local * heads_dev
    features = out_weight.shape[1]
    params = pltpu.CompilerParams(vmem_limit_bytes=24 * 1024 * 1024)
    shape = jax.ShapeDtypeStruct

    flat_query = query.reshape(rows, head_dim)
    copies = pl.pallas_call(
        copies_kernel,
        out_shape=shape((ring_z, rows, head_dim), bf16),
        in_specs=vmem(1),
        out_specs=vmem(1)[0],
        compiler_params=params,
        cost_estimate=pl.CostEstimate(flops=20_000_000_000, bytes_accessed=1_000_000, transcendentals=0),
        name="copies",
    )(flat_query)
    row = lax.all_to_all(copies, "z", 0, 0, tiled=True).reshape(ring_z * rows, head_dim)
    from_rows = {0: row}
    for k in (1, 3, 2):
        pairs = [(i, (i + k) % ring_y) for i in range(ring_y)]
        from_rows[k] = lax.ppermute(row, "y", pairs)
    keys = key_cache.reshape(slot_count, block_len, head_dim)
    values = value_cache.reshape(slot_count, block_len, head_dim)
    sent_rows = (lent_slots + 1) * heads_dev
    sent, local_out, local_note = pl.pallas_call(
        attend_kernel,
        out_shape=(
            shape((n_inst * sent_rows, head_dim), bf16),
            shape((slot_count, heads_dev, head_dim), f32),
            shape((slot_count // lent_slots, heads_dev, head_dim), f32),
        ),
        in_specs=smem(3) + vmem(6),
        out_specs=tuple(vmem(3)),
        scratch_shapes=[
            pltpu.VMEM((n_inst * lent_slots + 1, heads_dev, head_dim), f32),
            pltpu.VMEM((n_inst * lent_slots + 1, heads_dev, head_dim), f32),
            pltpu.SMEM((n_inst,), jnp.int32),
        ],
        compiler_params=params,
        name="attend",
    )(block_owner, block_index, lengths, *[from_rows[k] for k in range(ring_y)], keys, values)
    got = lax.all_to_all(
        sent.reshape(n_inst, sent_rows, head_dim), inst, 0, 0, tiled=True
    ).reshape(n_inst * sent_rows, head_dim)
    attended, for_core = pl.pallas_call(
        merge_kernel,
        out_shape=(
            shape((req_local, heads_dev * head_dim), bf16),
            shape((req_local, features // 2), bf16),
        ),
        in_specs=vmem(7),
        out_specs=tuple(vmem(2)),
        scratch_shapes=[pltpu.VMEM((req_local, heads_dev, head_dim), f32)],
        compiler_params=params,
        name="merge",
    )(
        got, local_out, local_note, flat_query,
        new_key.reshape(req_local, head_dim), new_value.reshape(req_local, head_dim), out_weight,
    )
    from_core = lax.ppermute(for_core, "tp", [(i, i ^ 1) for i in range(n_tp)])
    keep = pl.pallas_call(
        project_kernel,
        out_shape=shape((req_local, features // 2), f32),
        in_specs=vmem(2),
        out_specs=vmem(1)[0],
        compiler_params=params,
        cost_estimate=pl.CostEstimate(flops=200_000_000, bytes_accessed=4_000_000, transcendentals=0),
        name="project",
    )(attended, out_weight)
    width = features // n_tp
    own, *parts = pl.pallas_call(
        split_kernel,
        out_shape=(shape((req_local, width), f32),) + (shape((req_local, width), bf16),) * 3,
        in_specs=vmem(2),
        out_specs=tuple(vmem(4)),
        compiler_params=params,
        name="split",
    )(keep, from_core)
    total = own
    for k in (2, 1, 3):
        pairs = [(i, (i + 2 * k) % n_tp) for i in range(n_tp)]
        total = total + lax.ppermute(parts[k - 1], "tp", pairs).astype(f32)
    return total.astype(bf16)


def solution(mesh):
    shape = (ring_y, mesh.shape["inst"] // ring_y, mesh.shape["tp"])
    mesh = Mesh(mesh.devices.reshape(shape), ("y", "z", "tp"))
    placed = (
        P(inst, "tp", None),
        P(inst, "tp", None),
        P(inst, "tp", None),
        P(inst, None, "tp", None),
        P(inst, None, "tp", None),
        P("tp", None),
        P(),
        P(inst),
        P(inst),
    )
    return jax.shard_map(
        body, mesh=mesh, in_specs=placed, out_specs=P(inst, "tp"), check_vma=False
    )
```

```python
import jax
import jax.numpy as jnp
from jax import lax
from jax.experimental import pallas as pl
from jax.experimental.pallas import tpu as pltpu
from jax.sharding import Mesh
from jax.sharding import PartitionSpec as P

masked_score = -1e30
lent_slots = 4
inst = ("y", "z")
ring_y = 4
f32 = jnp.float32
bf16 = jnp.bfloat16


def copies_kernel(query_ref, copies_ref):
    for j in range(copies_ref.shape[0]):
        copies_ref[j] = query_ref[...]


def attend_kernel(
    owner_ref, index_ref, length_ref, row0_ref, row2_ref, row3_ref, row1_ref, key_ref, value_ref,
    sent_ref, local_out_ref, local_note_ref, entry_out, entry_note, used_count,
):
    slots, block_len, head_dim = key_ref.shape
    heads = 8
    row_refs = (row0_ref, row1_ref, row2_ref, row3_ref)
    row_requests = row0_ref.shape[0] // heads
    n_inst = ring_y * row_requests // 8
    spare = n_inst * lent_slots
    scale = head_dim ** (-0.5)
    my_row = lax.axis_index("y")
    me = lax.axis_index(inst)
    token = lax.broadcasted_iota(jnp.int32, (heads, block_len), 1)
    lane = lax.broadcasted_iota(jnp.int32, (heads, head_dim), 1)
    kind = lane % 4
    group = lane // 4
    blank = jnp.where(kind == 3, -1.0, 0.0).astype(f32)

    for e in range(spare):
        entry_out[e] = jnp.zeros((heads, head_dim), f32)
        entry_note[e] = blank
    for j in range(n_inst):
        used_count[j] = 0

    owners = [owner_ref[p] for p in range(slots)]
    holders = [jnp.maximum(o, 0) for o in owners]
    scores = []
    for p in range(slots):
        back = lax.rem(my_row + ring_y - holders[p] // row_requests, ring_y)
        at = pl.ds(pl.multiple_of((lax.rem(holders[p], row_requests) // 2) * 16, 16), 16)
        pair = row_refs[0][at, :]
        for k in range(1, ring_y):
            pair = jnp.where(back == k, row_refs[k][at, :], pair)
        both = lax.dot_general(
            pair, key_ref[p], (((1,), (1,)), ((), ())), preferred_element_type=f32
        )
        scores.append(jnp.where(holders[p] % 2 == 1, both[heads:], both[:heads]) * scale)
    notes = []
    for p in range(slots):
        limit = jnp.where(
            owners[p] >= 0, length_ref[holders[p]] - index_ref[p] * block_len, 0
        )
        live = token < limit
        score = jnp.where(live, scores[p], masked_score)
        top = jnp.max(score, axis=1, keepdims=True)
        top = (top + jnp.abs(top) * 0.0078125).astype(bf16).astype(f32)
        weight = jnp.where(live, jnp.exp(score - top), 0.0).astype(bf16)
        total = jnp.sum(weight.astype(f32), axis=1, keepdims=True)
        out = jnp.dot(weight, value_ref[p], preferred_element_type=f32)
        home = holders[p] // 8
        request = (holders[p] % 8).astype(f32)
        foreign = (owners[p] >= 0) & (home != me)
        local = (owners[p] >= 0) & (home == me)
        rank = used_count[home]
        used_count[home] = rank + foreign.astype(jnp.int32)
        place = jnp.where(foreign, home * lent_slots + rank, spare)
        high = total.astype(bf16).astype(f32)
        note = jnp.where(kind == 0, top, jnp.where(kind == 1, high, total - high))
        entry_out[place] = out
        entry_note[place] = jnp.where(kind == 3, request, note)
        local_out_ref[p] = out
        notes.append(jnp.where(kind == 3, jnp.where(local, request, -1.0), note))
        if p % 4 == 3:
            a, b, c, d = notes[p - 3 : p + 1]
            local_note_ref[p // 4] = jnp.where(
                group == 0, a, jnp.where(group == 1, b, jnp.where(group == 2, c, d))
            )
    for jj in range(n_inst // 2):
        rows = []
        for j in (2 * jj, 2 * jj + 1):
            a, b, c, d = [entry_note[j * lent_slots + k] for k in range(lent_slots)]
            rows += [entry_out[j * lent_slots + k] for k in range(lent_slots)]
            rows.append(
                jnp.where(group == 0, a, jnp.where(group == 1, b, jnp.where(group == 2, c, d)))
            )
        sent_ref[pl.ds(80 * jj, 80), :] = jnp.concatenate(rows, axis=0).astype(bf16)


def merge_kernel(
    got_ref, local_out_ref, local_note_ref, query_ref, new_key_ref, new_value_ref, weight_ref,
    attended_ref, send_ref, attended_rows,
):
    heads = 8
    rows, head_dim = query_ref.shape
    requests = rows // heads
    scale = head_dim ** (-0.5)
    outs, notes = [], []
    for jj in range(got_ref.shape[0] // 80):
        block = got_ref[pl.ds(80 * jj, 80), :].astype(f32)
        for start in (0, 40):
            outs.append([block[start + 8 * k : start + 8 * k + 8] for k in range(lent_slots)])
            notes.append(block[start + 32 : start + 40])
    for g in range(local_note_ref.shape[0]):
        outs.append([local_out_ref[4 * g + k] for k in range(lent_slots)])
        notes.append(local_note_ref[g])
    while len(notes) % 16:
        outs.append([jnp.zeros((heads, head_dim), f32)] * lent_slots)
        notes.append(jnp.full((heads, head_dim), -1.0, f32))
    turned = jnp.concatenate(
        [jnp.concatenate(notes[g : g + 16], axis=0).T[:16] for g in range(0, len(notes), 16)], axis=1
    )
    entries = turned.shape[1]
    head_of = lax.broadcasted_iota(jnp.int32, (1, entries), 1) % heads
    row_id = lax.broadcasted_iota(jnp.int32, (rows, entries), 0).astype(f32)

    spread = (requests, heads, head_dim)
    new_key = jnp.broadcast_to(new_key_ref[...].astype(f32)[:, None, :], spread).reshape(rows, head_dim)
    new_value = jnp.broadcast_to(new_value_ref[...].astype(f32)[:, None, :], spread).reshape(rows, head_dim)
    own = jnp.sum(query_ref[...].astype(f32) * new_key, axis=1, keepdims=True) * scale

    tops = []
    for k in range(lent_slots):
        whose = turned[4 * k + 3 : 4 * k + 4] * heads + head_of.astype(f32)
        tops.append(jnp.where(row_id == whose, turned[4 * k : 4 * k + 1], masked_score))
    most = jnp.maximum(jnp.maximum(tops[0], tops[1]), jnp.maximum(tops[2], tops[3]))
    top = jnp.maximum(jnp.max(most, axis=1, keepdims=True), own)
    own_weight = jnp.exp(own - top).astype(bf16).astype(f32)
    total = 0.0
    value = own_weight * new_value
    for k in range(lent_slots):
        factor = jnp.exp(tops[k] - top).astype(bf16)
        sums = turned[4 * k + 1 : 4 * k + 2] + turned[4 * k + 2 : 4 * k + 3]
        total = total + factor.astype(f32) * sums
        part = jnp.concatenate([out[k] for out in outs], axis=0).astype(bf16)
        value = value + jnp.dot(factor, part, preferred_element_type=f32)
    total = jnp.sum(total, axis=1, keepdims=True) + own_weight
    attended_rows[...] = (value / total).reshape(spread)
    attended = jnp.concatenate([attended_rows[:, h, :] for h in range(heads)], axis=1).astype(bf16)
    attended_ref[...] = attended
    other = 1 - lax.axis_index("tp") % 2
    width = send_ref.shape[1] // 4
    for n in range(4):
        at = pl.ds(pl.multiple_of((2 * n + other) * width, width), width)
        send_ref[:, n * width : (n + 1) * width] = jnp.dot(
            attended, weight_ref[:, at], preferred_element_type=f32
        ).astype(bf16)


def project_kernel(attended_ref, weight_ref, keep_ref):
    mine = lax.axis_index("tp") % 2
    width = keep_ref.shape[1] // 4
    attended = attended_ref[...]
    for n in range(4):
        at = pl.ds(pl.multiple_of((2 * n + mine) * width, width), width)
        keep_ref[:, n * width : (n + 1) * width] = jnp.dot(
            attended, weight_ref[:, at], preferred_element_type=f32
        )


def split_kernel(keep_ref, got_ref, own_ref, *send_refs):
    chip = lax.axis_index("tp") // 2
    width = own_ref.shape[1]
    for k in range(4):
        at = pl.ds(pl.multiple_of(lax.rem(chip + k, 4) * width, width), width)
        total = keep_ref[:, at] + got_ref[:, at].astype(f32)
        if k == 0:
            own_ref[...] = total
        else:
            send_refs[k - 1][...] = total.astype(bf16)


def vmem(n):
    return [pl.BlockSpec(memory_space=pltpu.VMEM)] * n


def smem(n):
    return [pl.BlockSpec(memory_space=pltpu.SMEM)] * n


def body(
    query, new_key, new_value, key_cache, value_cache, out_weight, lengths, block_owner, block_index
):
    req_local, heads_dev, head_dim = query.shape
    slot_count, block_len, _, _ = key_cache.shape
    n_inst = lengths.shape[0] // req_local
    ring_z = n_inst // ring_y
    n_tp = lax.axis_size("tp")
    rows = req_local * heads_dev
    features = out_weight.shape[1]
    params = pltpu.CompilerParams(vmem_limit_bytes=24 * 1024 * 1024)
    shape = jax.ShapeDtypeStruct

    flat_query = query.reshape(rows, head_dim)
    copies = pl.pallas_call(
        copies_kernel,
        out_shape=shape((ring_z, rows, head_dim), bf16),
        in_specs=vmem(1),
        out_specs=vmem(1)[0],
        compiler_params=params,
        cost_estimate=pl.CostEstimate(flops=20_000_000_000, bytes_accessed=1_000_000, transcendentals=0),
        name="copies",
    )(flat_query)
    row = lax.all_to_all(copies, "z", 0, 0, tiled=True).reshape(ring_z * rows, head_dim)
    from_rows = {0: row}
    for k in (1, 3, 2):
        pairs = [(i, (i + k) % ring_y) for i in range(ring_y)]
        from_rows[k] = lax.ppermute(row, "y", pairs)
    keys = key_cache.reshape(slot_count, block_len, head_dim)
    values = value_cache.reshape(slot_count, block_len, head_dim)
    sent_rows = (lent_slots + 1) * heads_dev
    sent, local_out, local_note = pl.pallas_call(
        attend_kernel,
        out_shape=(
            shape((n_inst * sent_rows, head_dim), bf16),
            shape((slot_count, heads_dev, head_dim), f32),
            shape((slot_count // lent_slots, heads_dev, head_dim), f32),
        ),
        in_specs=smem(3) + vmem(6),
        out_specs=tuple(vmem(3)),
        scratch_shapes=[
            pltpu.VMEM((n_inst * lent_slots + 1, heads_dev, head_dim), f32),
            pltpu.VMEM((n_inst * lent_slots + 1, heads_dev, head_dim), f32),
            pltpu.SMEM((n_inst,), jnp.int32),
        ],
        compiler_params=params,
        name="attend",
    )(block_owner, block_index, lengths, *[from_rows[k] for k in (0, 2, 3, 1)], keys, values)
    got = lax.all_to_all(
        sent.reshape(n_inst, sent_rows, head_dim), inst, 0, 0, tiled=True
    ).reshape(n_inst * sent_rows, head_dim)
    attended, for_core = pl.pallas_call(
        merge_kernel,
        out_shape=(
            shape((req_local, heads_dev * head_dim), bf16),
            shape((req_local, features // 2), bf16),
        ),
        in_specs=vmem(7),
        out_specs=tuple(vmem(2)),
        scratch_shapes=[pltpu.VMEM((req_local, heads_dev, head_dim), f32)],
        compiler_params=params,
        name="merge",
    )(
        got, local_out, local_note, flat_query,
        new_key.reshape(req_local, head_dim), new_value.reshape(req_local, head_dim), out_weight,
    )
    from_core = lax.ppermute(for_core, "tp", [(i, i ^ 1) for i in range(n_tp)])
    keep = pl.pallas_call(
        project_kernel,
        out_shape=shape((req_local, features // 2), f32),
        in_specs=vmem(2),
        out_specs=vmem(1)[0],
        compiler_params=params,
        cost_estimate=pl.CostEstimate(flops=200_000_000, bytes_accessed=4_000_000, transcendentals=0),
        name="project",
    )(attended, out_weight)
    width = features // n_tp
    own, *parts = pl.pallas_call(
        split_kernel,
        out_shape=(shape((req_local, width), f32),) + (shape((req_local, width), bf16),) * 3,
        in_specs=vmem(2),
        out_specs=tuple(vmem(4)),
        compiler_params=params,
        name="split",
    )(keep, from_core)
    total = own
    for k in (2, 1, 3):
        pairs = [(i, (i + 2 * k) % n_tp) for i in range(n_tp)]
        total = total + lax.ppermute(parts[k - 1], "tp", pairs).astype(f32)
    return total.astype(bf16)


def solution(mesh):
    shape = (ring_y, mesh.shape["inst"] // ring_y, mesh.shape["tp"])
    mesh = Mesh(mesh.devices.reshape(shape), ("y", "z", "tp"))
    placed = (
        P(inst, "tp", None),
        P(inst, "tp", None),
        P(inst, "tp", None),
        P(inst, None, "tp", None),
        P(inst, None, "tp", None),
        P("tp", None),
        P(),
        P(inst),
        P(inst),
    )
    return jax.shard_map(
        body, mesh=mesh, in_specs=placed, out_specs=P(inst, "tp"), check_vma=False
    )
```

```python
import jax
import jax.numpy as jnp
from jax import lax
from jax.experimental import pallas as pl
from jax.experimental.pallas import tpu as pltpu
from jax.sharding import Mesh
from jax.sharding import PartitionSpec as P

masked_score = -1e30
lent_slots = 4
inst = ("y", "z")
ring_y = 4
f32 = jnp.float32
bf16 = jnp.bfloat16


def copies_kernel(query_ref, copies_ref):
    for j in range(copies_ref.shape[0]):
        copies_ref[j] = query_ref[...]


def plan_kernel(
    owner_ref, index_ref, length_ref, row_ref, place_ref, limit_ref, sent_id_ref, local_id_ref,
    used_count,
):
    slots, lanes = place_ref.shape
    row_requests = row_ref.shape[0] // 8
    n_inst = ring_y * row_requests // 8
    block_len = 256
    my_row = lax.axis_index("y")
    me = lax.axis_index(inst)
    lane = lax.broadcasted_iota(jnp.int32, (1, lanes), 1)
    for j in range(n_inst):
        used_count[j] = 0
    for p in range(slots):
        owner = owner_ref[p]
        holder = jnp.maximum(owner, 0)
        home = holder // 8
        back = lax.rem(my_row + ring_y - holder // row_requests, ring_y)
        source = back * row_requests + lax.rem(holder, row_requests)
        foreign = (owner >= 0) & (home != me)
        local = (owner >= 0) & (home == me)
        rank = used_count[home]
        used_count[home] = rank + foreign.astype(jnp.int32)
        place = jnp.where(foreign, home * lent_slots + rank, n_inst * lent_slots)
        limit = jnp.where(owner >= 0, length_ref[holder] - index_ref[p] * block_len, 0)
        request = (holder % 8).astype(f32)
        place_ref[p : p + 1, :] = jnp.where(lane == 0, source, place)
        limit_ref[p : p + 1, :] = jnp.full((1, lanes), limit, jnp.int32)
        sent_id_ref[p : p + 1, :] = jnp.full((1, lanes), request, f32)
        local_id_ref[p : p + 1, :] = jnp.full((1, lanes), jnp.where(local, request, -1.0), f32)


def attend_kernel(
    place_ref, limit_ref, sent_id_ref, local_id_ref, row0_ref, row2_ref, row3_ref, row1_ref,
    key_ref, value_ref, sent_ref, local_out_ref, local_note_ref, entry_out, entry_note,
):
    slots, block_len, head_dim = key_ref.shape
    heads = 8
    row_refs = (row0_ref, row1_ref, row2_ref, row3_ref)
    row_requests = row0_ref.shape[0] // heads
    n_inst = ring_y * row_requests // 8
    spare = n_inst * lent_slots
    scale = head_dim ** (-0.5)
    token = lax.broadcasted_iota(jnp.int32, (heads, block_len), 1)
    lane = lax.broadcasted_iota(jnp.int32, (heads, head_dim), 1)
    kind = lane % 4
    group = lane // 4
    blank = jnp.where(kind == 3, -1.0, 0.0).astype(f32)

    for e in range(spare):
        entry_out[e] = jnp.zeros((heads, head_dim), f32)
        entry_note[e] = blank

    scores = []
    for p in range(slots):
        source = place_ref[p, 0]
        at = pl.ds(pl.multiple_of((lax.rem(source, row_requests) // 2) * 16, 16), 16)
        pair = row_refs[0][at, :]
        for k in range(1, ring_y):
            pair = jnp.where(source // row_requests == k, row_refs[k][at, :], pair)
        both = lax.dot_general(
            pair, key_ref[p], (((1,), (1,)), ((), ())), preferred_element_type=f32
        )
        scores.append(jnp.where(source % 2 == 1, both[heads:], both[:heads]) * scale)
    notes = []
    for p in range(slots):
        limit = jnp.broadcast_to(limit_ref[p : p + 1, :], (heads, head_dim))
        limit = jnp.concatenate([limit] * (block_len // head_dim), axis=1)
        live = token < limit
        score = jnp.where(live, scores[p], masked_score)
        top = jnp.max(score, axis=1, keepdims=True)
        top = (top + jnp.abs(top) * 0.0078125).astype(bf16).astype(f32)
        weight = jnp.where(live, jnp.exp(score - top), 0.0).astype(bf16)
        total = jnp.sum(weight.astype(f32), axis=1, keepdims=True)
        out = jnp.dot(weight, value_ref[p], preferred_element_type=f32)
        place = place_ref[p, 1]
        high = total.astype(bf16).astype(f32)
        note = jnp.where(kind == 0, top, jnp.where(kind == 1, high, total - high))
        entry_out[place] = out
        entry_note[place] = jnp.where(kind == 3, sent_id_ref[p : p + 1, :], note)
        local_out_ref[p] = out
        notes.append(jnp.where(kind == 3, local_id_ref[p : p + 1, :], note))
        if p % 4 == 3:
            a, b, c, d = notes[p - 3 : p + 1]
            local_note_ref[p // 4] = jnp.where(
                group == 0, a, jnp.where(group == 1, b, jnp.where(group == 2, c, d))
            )
    for jj in range(n_inst // 2):
        rows = []
        for j in (2 * jj, 2 * jj + 1):
            a, b, c, d = [entry_note[j * lent_slots + k] for k in range(lent_slots)]
            rows += [entry_out[j * lent_slots + k] for k in range(lent_slots)]
            rows.append(
                jnp.where(group == 0, a, jnp.where(group == 1, b, jnp.where(group == 2, c, d)))
            )
        sent_ref[pl.ds(80 * jj, 80), :] = jnp.concatenate(rows, axis=0).astype(bf16)


def merge_kernel(
    got_ref, local_out_ref, local_note_ref, query_ref, new_key_ref, new_value_ref, weight_ref,
    attended_ref, send_ref, attended_rows,
):
    heads = 8
    rows, head_dim = query_ref.shape
    requests = rows // heads
    scale = head_dim ** (-0.5)
    outs, notes = [], []
    for jj in range(got_ref.shape[0] // 80):
        block = got_ref[pl.ds(80 * jj, 80), :].astype(f32)
        for start in (0, 40):
            outs.append([block[start + 8 * k : start + 8 * k + 8] for k in range(lent_slots)])
            notes.append(block[start + 32 : start + 40])
    for g in range(local_note_ref.shape[0]):
        outs.append([local_out_ref[4 * g + k] for k in range(lent_slots)])
        notes.append(local_note_ref[g])
    while len(notes) % 16:
        outs.append([jnp.zeros((heads, head_dim), f32)] * lent_slots)
        notes.append(jnp.full((heads, head_dim), -1.0, f32))
    turned = jnp.concatenate(
        [jnp.concatenate(notes[g : g + 16], axis=0).T[:16] for g in range(0, len(notes), 16)], axis=1
    )
    entries = turned.shape[1]
    head_of = lax.broadcasted_iota(jnp.int32, (1, entries), 1) % heads
    row_id = lax.broadcasted_iota(jnp.int32, (rows, entries), 0).astype(f32)

    spread = (requests, heads, head_dim)
    new_key = jnp.broadcast_to(new_key_ref[...].astype(f32)[:, None, :], spread).reshape(rows, head_dim)
    new_value = jnp.broadcast_to(new_value_ref[...].astype(f32)[:, None, :], spread).reshape(rows, head_dim)
    own = jnp.sum(query_ref[...].astype(f32) * new_key, axis=1, keepdims=True) * scale

    tops = []
    for k in range(lent_slots):
        whose = turned[4 * k + 3 : 4 * k + 4] * heads + head_of.astype(f32)
        tops.append(jnp.where(row_id == whose, turned[4 * k : 4 * k + 1], masked_score))
    most = jnp.maximum(jnp.maximum(tops[0], tops[1]), jnp.maximum(tops[2], tops[3]))
    top = jnp.maximum(jnp.max(most, axis=1, keepdims=True), own)
    own_weight = jnp.exp(own - top).astype(bf16).astype(f32)
    total = 0.0
    value = own_weight * new_value
    for k in range(lent_slots):
        factor = jnp.exp(tops[k] - top).astype(bf16)
        sums = turned[4 * k + 1 : 4 * k + 2] + turned[4 * k + 2 : 4 * k + 3]
        total = total + factor.astype(f32) * sums
        part = jnp.concatenate([out[k] for out in outs], axis=0).astype(bf16)
        value = value + jnp.dot(factor, part, preferred_element_type=f32)
    total = jnp.sum(total, axis=1, keepdims=True) + own_weight
    attended_rows[...] = (value / total).reshape(spread)
    attended = jnp.concatenate([attended_rows[:, h, :] for h in range(heads)], axis=1).astype(bf16)
    attended_ref[...] = attended
    other = 1 - lax.axis_index("tp") % 2
    width = send_ref.shape[1] // 4
    for n in range(4):
        at = pl.ds(pl.multiple_of((2 * n + other) * width, width), width)
        send_ref[:, n * width : (n + 1) * width] = jnp.dot(
            attended, weight_ref[:, at], preferred_element_type=f32
        ).astype(bf16)


def project_kernel(attended_ref, weight_ref, keep_ref):
    mine = lax.axis_index("tp") % 2
    width = keep_ref.shape[1] // 4
    attended = attended_ref[...]
    for n in range(4):
        at = pl.ds(pl.multiple_of((2 * n + mine) * width, width), width)
        keep_ref[:, n * width : (n + 1) * width] = jnp.dot(
            attended, weight_ref[:, at], preferred_element_type=f32
        )


def split_kernel(keep_ref, got_ref, own_ref, *send_refs):
    chip = lax.axis_index("tp") // 2
    width = own_ref.shape[1]
    for k in range(4):
        at = pl.ds(pl.multiple_of(lax.rem(chip + k, 4) * width, width), width)
        total = keep_ref[:, at] + got_ref[:, at].astype(f32)
        if k == 0:
            own_ref[...] = total
        else:
            send_refs[k - 1][...] = total.astype(bf16)


def vmem(n):
    return [pl.BlockSpec(memory_space=pltpu.VMEM)] * n


def smem(n):
    return [pl.BlockSpec(memory_space=pltpu.SMEM)] * n


def body(
    query, new_key, new_value, key_cache, value_cache, out_weight, lengths, block_owner, block_index
):
    req_local, heads_dev, head_dim = query.shape
    slot_count, block_len, _, _ = key_cache.shape
    n_inst = lengths.shape[0] // req_local
    ring_z = n_inst // ring_y
    n_tp = lax.axis_size("tp")
    rows = req_local * heads_dev
    features = out_weight.shape[1]
    params = pltpu.CompilerParams(vmem_limit_bytes=24 * 1024 * 1024)
    shape = jax.ShapeDtypeStruct

    flat_query = query.reshape(rows, head_dim)
    copies = pl.pallas_call(
        copies_kernel,
        out_shape=shape((ring_z, rows, head_dim), bf16),
        in_specs=vmem(1),
        out_specs=vmem(1)[0],
        compiler_params=params,
        cost_estimate=pl.CostEstimate(flops=20_000_000_000, bytes_accessed=1_000_000, transcendentals=0),
        name="copies",
    )(flat_query)
    row = lax.all_to_all(copies, "z", 0, 0, tiled=True).reshape(ring_z * rows, head_dim)
    from_rows = {0: row}
    for k in (1, 3, 2):
        pairs = [(i, (i + k) % ring_y) for i in range(ring_y)]
        from_rows[k] = lax.ppermute(row, "y", pairs)
    plan = pl.pallas_call(
        plan_kernel,
        out_shape=(shape((slot_count, head_dim), jnp.int32),) * 2
        + (shape((slot_count, head_dim), f32),) * 2,
        in_specs=smem(3) + [pl.BlockSpec(memory_space=pl.ANY)],
        out_specs=tuple(vmem(4)),
        scratch_shapes=[pltpu.SMEM((n_inst,), jnp.int32)],
        compiler_params=params,
        cost_estimate=pl.CostEstimate(flops=2_000_000_000, bytes_accessed=100_000, transcendentals=0),
        name="plan",
    )(block_owner, block_index, lengths, row)
    keys = key_cache.reshape(slot_count, block_len, head_dim)
    values = value_cache.reshape(slot_count, block_len, head_dim)
    sent_rows = (lent_slots + 1) * heads_dev
    sent, local_out, local_note = pl.pallas_call(
        attend_kernel,
        out_shape=(
            shape((n_inst * sent_rows, head_dim), bf16),
            shape((slot_count, heads_dev, head_dim), f32),
            shape((slot_count // lent_slots, heads_dev, head_dim), f32),
        ),
        in_specs=vmem(10),
        out_specs=tuple(vmem(3)),
        scratch_shapes=[
            pltpu.VMEM((n_inst * lent_slots + 1, heads_dev, head_dim), f32),
            pltpu.VMEM((n_inst * lent_slots + 1, heads_dev, head_dim), f32),
        ],
        compiler_params=params,
        name="attend",
    )(*plan, *[from_rows[k] for k in (0, 2, 3, 1)], keys, values)
    got = lax.all_to_all(
        sent.reshape(n_inst, sent_rows, head_dim), inst, 0, 0, tiled=True
    ).reshape(n_inst * sent_rows, head_dim)
    attended, for_core = pl.pallas_call(
        merge_kernel,
        out_shape=(
            shape((req_local, heads_dev * head_dim), bf16),
            shape((req_local, features // 2), bf16),
        ),
        in_specs=vmem(7),
        out_specs=tuple(vmem(2)),
        scratch_shapes=[pltpu.VMEM((req_local, heads_dev, head_dim), f32)],
        compiler_params=params,
        name="merge",
    )(
        got, local_out, local_note, flat_query,
        new_key.reshape(req_local, head_dim), new_value.reshape(req_local, head_dim), out_weight,
    )
    from_core = lax.ppermute(for_core, "tp", [(i, i ^ 1) for i in range(n_tp)])
    keep = pl.pallas_call(
        project_kernel,
        out_shape=shape((req_local, features // 2), f32),
        in_specs=vmem(2),
        out_specs=vmem(1)[0],
        compiler_params=params,
        cost_estimate=pl.CostEstimate(flops=200_000_000, bytes_accessed=4_000_000, transcendentals=0),
        name="project",
    )(attended, out_weight)
    width = features // n_tp
    own, *parts = pl.pallas_call(
        split_kernel,
        out_shape=(shape((req_local, width), f32),) + (shape((req_local, width), bf16),) * 3,
        in_specs=vmem(2),
        out_specs=tuple(vmem(4)),
        compiler_params=params,
        name="split",
    )(keep, from_core)
    total = own
    for k in (2, 1, 3):
        pairs = [(i, (i + 2 * k) % n_tp) for i in range(n_tp)]
        total = total + lax.ppermute(parts[k - 1], "tp", pairs).astype(f32)
    return total.astype(bf16)


def solution(mesh):
    shape = (ring_y, mesh.shape["inst"] // ring_y, mesh.shape["tp"])
    mesh = Mesh(mesh.devices.reshape(shape), ("y", "z", "tp"))
    placed = (
        P(inst, "tp", None),
        P(inst, "tp", None),
        P(inst, "tp", None),
        P(inst, None, "tp", None),
        P(inst, None, "tp", None),
        P("tp", None),
        P(),
        P(inst),
        P(inst),
    )
    return jax.shard_map(
        body, mesh=mesh, in_specs=placed, out_specs=P(inst, "tp"), check_vma=False
    )
```

```python
import jax
import jax.numpy as jnp
from jax import lax
from jax.experimental import pallas as pl
from jax.experimental.pallas import tpu as pltpu
from jax.sharding import Mesh
from jax.sharding import PartitionSpec as P

masked_score = -1e30
lent_slots = 4
inst = ("y", "z")
ring_y = 4
f32 = jnp.float32
bf16 = jnp.bfloat16


def copies_kernel(query_ref, copies_ref):
    for j in range(copies_ref.shape[0]):
        copies_ref[j] = query_ref[...]


def plan_kernel(
    owner_ref, index_ref, length_ref, row_ref, place_ref, limit_ref, sent_id_ref, local_id_ref,
    used_count,
):
    slots, lanes = place_ref.shape
    row_requests = row_ref.shape[0] // 8
    n_inst = ring_y * row_requests // 8
    block_len = 256
    my_row = lax.axis_index("y")
    me = lax.axis_index(inst)
    lane = lax.broadcasted_iota(jnp.int32, (1, lanes), 1)
    for j in range(n_inst):
        used_count[j] = 0
    for p in range(slots):
        owner = owner_ref[p]
        holder = jnp.maximum(owner, 0)
        home = holder // 8
        back = lax.rem(my_row + ring_y - holder // row_requests, ring_y)
        source = back * row_requests + lax.rem(holder, row_requests)
        foreign = (owner >= 0) & (home != me)
        local = (owner >= 0) & (home == me)
        rank = used_count[home]
        used_count[home] = rank + foreign.astype(jnp.int32)
        place = jnp.where(foreign, home * lent_slots + rank, n_inst * lent_slots)
        limit = jnp.where(owner >= 0, length_ref[holder] - index_ref[p] * block_len, 0)
        request = (holder % 8).astype(f32)
        place_ref[p : p + 1, :] = jnp.where(lane == 0, source, place)
        limit_ref[p : p + 1, :] = jnp.full((1, lanes), limit, jnp.int32)
        sent_id_ref[p : p + 1, :] = jnp.full((1, lanes), request, f32)
        local_id_ref[p : p + 1, :] = jnp.full((1, lanes), jnp.where(local, request, -1.0), f32)


def attend_kernel(
    place_ref, limit_ref, sent_id_ref, local_id_ref, row0_ref, row2_ref, row3_ref, row1_ref,
    key_ref, value_ref, sent_ref, local_out_ref, local_note_ref, entry_out, entry_note,
):
    slots, block_len, head_dim = key_ref.shape
    heads = 8
    row_refs = (row0_ref, row1_ref, row2_ref, row3_ref)
    row_requests = row0_ref.shape[0] // heads
    n_inst = ring_y * row_requests // 8
    spare = n_inst * lent_slots
    scale = head_dim ** (-0.5)
    token = lax.broadcasted_iota(jnp.int32, (heads, block_len), 1)
    lane = lax.broadcasted_iota(jnp.int32, (heads, head_dim), 1)
    kind = lane % 4
    group = lane // 4
    blank = jnp.where(kind == 3, -1.0, 0.0).astype(f32)

    for e in range(spare):
        entry_out[e] = jnp.zeros((heads, head_dim), f32)
        entry_note[e] = blank

    scores = []
    for p in range(slots):
        source = place_ref[p, 0]
        at = pl.ds(pl.multiple_of((lax.rem(source, row_requests) // 2) * 16, 16), 16)
        pair = row_refs[0][at, :]
        for k in range(1, ring_y):
            pair = jnp.where(source // row_requests == k, row_refs[k][at, :], pair)
        both = lax.dot_general(
            pair, key_ref[p], (((1,), (1,)), ((), ())), preferred_element_type=f32
        )
        scores.append(jnp.where(source % 2 == 1, both[heads:], both[:heads]) * scale)
    notes = []
    for p in range(slots):
        limit = jnp.broadcast_to(limit_ref[p : p + 1, :], (heads, head_dim))
        limit = jnp.concatenate([limit] * (block_len // head_dim), axis=1)
        live = token < limit
        score = jnp.where(live, scores[p], masked_score)
        top = jnp.max(score, axis=1, keepdims=True)
        top = (top + jnp.abs(top) * 0.0078125).astype(bf16).astype(f32)
        weight = jnp.where(live, jnp.exp(score - top), 0.0).astype(bf16)
        total = jnp.sum(weight.astype(f32), axis=1, keepdims=True)
        out = jnp.dot(weight, value_ref[p], preferred_element_type=f32)
        place = place_ref[p, 1]
        high = total.astype(bf16).astype(f32)
        note = jnp.where(kind == 0, top, jnp.where(kind == 1, high, total - high))
        entry_out[place] = out
        entry_note[place] = jnp.where(kind == 3, sent_id_ref[p : p + 1, :], note)
        local_out_ref[p] = out
        notes.append(jnp.where(kind == 3, local_id_ref[p : p + 1, :], note))
        if p % 4 == 3:
            a, b, c, d = notes[p - 3 : p + 1]
            local_note_ref[p // 4] = jnp.where(
                group == 0, a, jnp.where(group == 1, b, jnp.where(group == 2, c, d))
            )
    for jj in range(n_inst // 2):
        rows = []
        for j in (2 * jj, 2 * jj + 1):
            a, b, c, d = [entry_note[j * lent_slots + k] for k in range(lent_slots)]
            rows += [entry_out[j * lent_slots + k] for k in range(lent_slots)]
            rows.append(
                jnp.where(group == 0, a, jnp.where(group == 1, b, jnp.where(group == 2, c, d)))
            )
        sent_ref[pl.ds(80 * jj, 80), :] = jnp.concatenate(rows, axis=0).astype(bf16)


def merge_kernel(
    got_ref, local_out_ref, local_note_ref, query_ref, new_key_ref, new_value_ref, weight_ref,
    attended_ref, send_ref, attended_rows,
):
    heads = 8
    rows, head_dim = query_ref.shape
    requests = rows // heads
    scale = head_dim ** (-0.5)
    outs, notes = [], []
    for jj in range(got_ref.shape[0] // 80):
        block = got_ref[pl.ds(80 * jj, 80), :].astype(f32)
        for start in (0, 40):
            outs.append([block[start + 8 * k : start + 8 * k + 8] for k in range(lent_slots)])
            notes.append(block[start + 32 : start + 40])
    for g in range(local_note_ref.shape[0]):
        outs.append([local_out_ref[4 * g + k] for k in range(lent_slots)])
        notes.append(local_note_ref[g])
    while len(notes) % 16:
        outs.append([jnp.zeros((heads, head_dim), f32)] * lent_slots)
        notes.append(jnp.full((heads, head_dim), -1.0, f32))
    turned = jnp.concatenate(
        [jnp.concatenate(notes[g : g + 16], axis=0).T[:16] for g in range(0, len(notes), 16)], axis=1
    )
    entries = turned.shape[1]
    head_of = lax.broadcasted_iota(jnp.int32, (1, entries), 1) % heads
    row_id = lax.broadcasted_iota(jnp.int32, (rows, entries), 0).astype(f32)

    spread = (requests, heads, head_dim)
    new_key = jnp.broadcast_to(new_key_ref[...].astype(f32)[:, None, :], spread).reshape(rows, head_dim)
    new_value = jnp.broadcast_to(new_value_ref[...].astype(f32)[:, None, :], spread).reshape(rows, head_dim)
    own = jnp.sum(query_ref[...].astype(f32) * new_key, axis=1, keepdims=True) * scale

    tops = []
    for k in range(lent_slots):
        whose = turned[4 * k + 3 : 4 * k + 4] * heads + head_of.astype(f32)
        tops.append(jnp.where(row_id == whose, turned[4 * k : 4 * k + 1], masked_score))
    most = jnp.maximum(jnp.maximum(tops[0], tops[1]), jnp.maximum(tops[2], tops[3]))
    top = jnp.maximum(jnp.max(most, axis=1, keepdims=True), own)
    own_weight = jnp.exp(own - top).astype(bf16).astype(f32)
    total = 0.0
    value = own_weight * new_value
    for k in range(lent_slots):
        factor = jnp.exp(tops[k] - top).astype(bf16)
        sums = turned[4 * k + 1 : 4 * k + 2] + turned[4 * k + 2 : 4 * k + 3]
        total = total + factor.astype(f32) * sums
        part = jnp.concatenate([out[k] for out in outs], axis=0).astype(bf16)
        value = value + jnp.dot(factor, part, preferred_element_type=f32)
    total = jnp.sum(total, axis=1, keepdims=True) + own_weight
    attended_rows[...] = (value / total).reshape(spread)
    attended = jnp.concatenate([attended_rows[:, h, :] for h in range(heads)], axis=1).astype(bf16)
    attended_ref[...] = attended
    other = 1 - lax.axis_index("tp") % 2
    width = send_ref.shape[1] // 4
    for n in range(4):
        at = pl.ds(pl.multiple_of((2 * n + other) * width, width), width)
        send_ref[:, n * width : (n + 1) * width] = jnp.dot(
            attended, weight_ref[:, at], preferred_element_type=f32
        ).astype(bf16)


def project_kernel(attended_ref, weight_ref, keep_ref):
    mine = lax.axis_index("tp") % 2
    width = keep_ref.shape[1] // 4
    attended = attended_ref[...]
    for n in range(4):
        at = pl.ds(pl.multiple_of((2 * n + mine) * width, width), width)
        keep_ref[:, n * width : (n + 1) * width] = jnp.dot(
            attended, weight_ref[:, at], preferred_element_type=f32
        )


def split_kernel(keep_ref, got_ref, own_ref, *send_refs):
    chip = lax.axis_index("tp") // 2
    width = own_ref.shape[1]
    for k in range(4):
        at = pl.ds(pl.multiple_of(lax.rem(chip + k, 4) * width, width), width)
        total = keep_ref[:, at] + got_ref[:, at].astype(f32)
        if k == 0:
            own_ref[...] = total
        else:
            send_refs[k - 1][...] = total.astype(bf16)


def vmem(n):
    return [pl.BlockSpec(memory_space=pltpu.VMEM)] * n


def smem(n):
    return [pl.BlockSpec(memory_space=pltpu.SMEM)] * n


def body(
    query, new_key, new_value, key_cache, value_cache, out_weight, lengths, block_owner, block_index
):
    req_local, heads_dev, head_dim = query.shape
    slot_count, block_len, _, _ = key_cache.shape
    n_inst = lengths.shape[0] // req_local
    ring_z = n_inst // ring_y
    n_tp = lax.axis_size("tp")
    rows = req_local * heads_dev
    features = out_weight.shape[1]
    params = pltpu.CompilerParams(vmem_limit_bytes=24 * 1024 * 1024)
    shape = jax.ShapeDtypeStruct

    flat_query = query.reshape(rows, head_dim)
    copies = pl.pallas_call(
        copies_kernel,
        out_shape=shape((ring_z, rows, head_dim), bf16),
        in_specs=vmem(1),
        out_specs=vmem(1)[0],
        compiler_params=params,
        cost_estimate=pl.CostEstimate(flops=20_000_000_000, bytes_accessed=1_000_000, transcendentals=0),
        name="copies",
    )(flat_query)
    row = lax.all_to_all(copies, "z", 0, 0, tiled=True).reshape(ring_z * rows, head_dim)
    from_rows = {0: row}
    for k in (1, 3, 2):
        pairs = [(i, (i + k) % ring_y) for i in range(ring_y)]
        from_rows[k] = lax.ppermute(row, "y", pairs)
    plan = pl.pallas_call(
        plan_kernel,
        out_shape=(shape((slot_count, head_dim), jnp.int32),) * 2
        + (shape((slot_count, head_dim), f32),) * 2,
        in_specs=smem(3) + [pl.BlockSpec(memory_space=pl.ANY)],
        out_specs=tuple(vmem(4)),
        scratch_shapes=[pltpu.SMEM((n_inst,), jnp.int32)],
        compiler_params=params,
        cost_estimate=pl.CostEstimate(flops=2_000_000_000, bytes_accessed=100_000, transcendentals=0),
        name="plan",
    )(block_owner, block_index, lengths, row)
    keys = key_cache.reshape(slot_count, block_len, head_dim)
    values = value_cache.reshape(slot_count, block_len, head_dim)
    sent_rows = (lent_slots + 1) * heads_dev
    sent, local_out, local_note = pl.pallas_call(
        attend_kernel,
        out_shape=(
            shape((n_inst * sent_rows, head_dim), bf16),
            shape((slot_count, heads_dev, head_dim), f32),
            shape((slot_count // lent_slots, heads_dev, head_dim), f32),
        ),
        in_specs=vmem(10),
        out_specs=tuple(vmem(3)),
        scratch_shapes=[
            pltpu.VMEM((n_inst * lent_slots + 1, heads_dev, head_dim), f32),
            pltpu.VMEM((n_inst * lent_slots + 1, heads_dev, head_dim), f32),
        ],
        compiler_params=params,
        name="attend",
    )(*plan, *[from_rows[k] for k in (0, 2, 3, 1)], keys, values)
    got = lax.all_to_all(
        sent.reshape(n_inst, sent_rows, head_dim), inst, 0, 0, tiled=True
    ).reshape(n_inst * sent_rows, head_dim)
    attended, for_core = pl.pallas_call(
        merge_kernel,
        out_shape=(
            shape((req_local, heads_dev * head_dim), bf16),
            shape((req_local, features // 2), bf16),
        ),
        in_specs=vmem(7),
        out_specs=tuple(vmem(2)),
        scratch_shapes=[pltpu.VMEM((req_local, heads_dev, head_dim), f32)],
        compiler_params=params,
        name="merge",
    )(
        got, local_out, local_note, flat_query,
        new_key.reshape(req_local, head_dim), new_value.reshape(req_local, head_dim), out_weight,
    )
    from_core = lax.ppermute(for_core, "tp", [(i, i ^ 1) for i in range(n_tp)])
    keep = pl.pallas_call(
        project_kernel,
        out_shape=shape((req_local, features // 2), f32),
        in_specs=vmem(2),
        out_specs=vmem(1)[0],
        compiler_params=params,
        cost_estimate=pl.CostEstimate(flops=200_000_000, bytes_accessed=4_000_000, transcendentals=0),
        name="project",
    )(attended, out_weight)
    width = features // n_tp
    own, *parts = pl.pallas_call(
        split_kernel,
        out_shape=(shape((req_local, width), f32),) + (shape((req_local, width), bf16),) * 3,
        in_specs=vmem(2),
        out_specs=tuple(vmem(4)),
        compiler_params=params,
        name="split",
    )(keep, from_core)
    total = own
    for k in (1, 2, 3):
        pairs = [(i, (i + 2 * k) % n_tp) for i in range(n_tp)]
        total = total + lax.ppermute(parts[k - 1], "tp", pairs).astype(f32)
    return total.astype(bf16)


def solution(mesh):
    shape = (ring_y, mesh.shape["inst"] // ring_y, mesh.shape["tp"])
    mesh = Mesh(mesh.devices.reshape(shape), ("y", "z", "tp"))
    placed = (
        P(inst, "tp", None),
        P(inst, "tp", None),
        P(inst, "tp", None),
        P(inst, None, "tp", None),
        P(inst, None, "tp", None),
        P("tp", None),
        P(),
        P(inst),
        P(inst),
    )
    return jax.shard_map(
        body, mesh=mesh, in_specs=placed, out_specs=P(inst, "tp"), check_vma=False
    )
```

```python
import jax
import jax.numpy as jnp
from jax import lax
from jax.experimental import pallas as pl
from jax.experimental.pallas import tpu as pltpu
from jax.sharding import Mesh
from jax.sharding import PartitionSpec as P

masked_score = -1e30
lent_slots = 4
inst = ("y", "z")
ring_y = 4
f32 = jnp.float32
bf16 = jnp.bfloat16


def copies_kernel(query_ref, copies_ref):
    for j in range(copies_ref.shape[0]):
        copies_ref[j] = query_ref[...]


def plan_kernel(
    owner_ref, index_ref, length_ref, row_ref, place_ref, limit_ref, sent_id_ref, local_id_ref,
    used_count,
):
    slots, lanes = place_ref.shape
    row_requests = row_ref.shape[0] // 8
    n_inst = ring_y * row_requests // 8
    block_len = 256
    my_row = lax.axis_index("y")
    me = lax.axis_index(inst)
    lane = lax.broadcasted_iota(jnp.int32, (1, lanes), 1)
    for j in range(n_inst):
        used_count[j] = 0
    for p in range(slots):
        owner = owner_ref[p]
        holder = jnp.maximum(owner, 0)
        home = holder // 8
        back = lax.rem(my_row + ring_y - holder // row_requests, ring_y)
        source = back * row_requests + lax.rem(holder, row_requests)
        foreign = (owner >= 0) & (home != me)
        local = (owner >= 0) & (home == me)
        rank = used_count[home]
        used_count[home] = rank + foreign.astype(jnp.int32)
        place = jnp.where(foreign, home * lent_slots + rank, n_inst * lent_slots)
        limit = jnp.where(owner >= 0, length_ref[holder] - index_ref[p] * block_len, 0)
        request = (holder % 8).astype(f32)
        place_ref[p : p + 1, :] = jnp.where(lane == 0, source, place)
        limit_ref[p : p + 1, :] = jnp.full((1, lanes), limit, jnp.int32)
        sent_id_ref[p : p + 1, :] = jnp.full((1, lanes), request, f32)
        local_id_ref[p : p + 1, :] = jnp.full((1, lanes), jnp.where(local, request, -1.0), f32)


def attend_kernel(
    place_ref, limit_ref, sent_id_ref, local_id_ref, row0_ref, row2_ref, row3_ref, row1_ref,
    key_ref, value_ref, sent_ref, local_out_ref, local_note_ref, entry_out, entry_note,
):
    slots, block_len, head_dim = key_ref.shape
    heads = 8
    row_refs = (row0_ref, row1_ref, row2_ref, row3_ref)
    row_requests = row0_ref.shape[0] // heads
    n_inst = ring_y * row_requests // 8
    spare = n_inst * lent_slots
    scale = head_dim ** (-0.5)
    token = lax.broadcasted_iota(jnp.int32, (heads, block_len), 1)
    lane = lax.broadcasted_iota(jnp.int32, (heads, head_dim), 1)
    kind = lane % 4
    group = lane // 4
    blank = jnp.where(kind == 3, -1.0, 0.0).astype(f32)

    for e in range(spare):
        entry_out[e] = jnp.zeros((heads, head_dim), f32)
        entry_note[e] = blank

    scores = []
    for p in range(slots):
        source = place_ref[p, 0]
        at = pl.ds(pl.multiple_of((lax.rem(source, row_requests) // 2) * 16, 16), 16)
        back = source // row_requests
        odd = lax.rem(back, 2) == 1
        near = jnp.where(odd, row_refs[1][at, :], row_refs[0][at, :])
        far = jnp.where(odd, row_refs[3][at, :], row_refs[2][at, :])
        pair = jnp.where(back >= 2, far, near)
        both = lax.dot_general(
            pair, key_ref[p], (((1,), (1,)), ((), ())), preferred_element_type=f32
        )
        scores.append(jnp.where(source % 2 == 1, both[heads:], both[:heads]) * scale)
    notes = []
    for p in range(slots):
        limit = jnp.broadcast_to(limit_ref[p : p + 1, :], (heads, head_dim))
        limit = jnp.concatenate([limit] * (block_len // head_dim), axis=1)
        live = token < limit
        score = jnp.where(live, scores[p], masked_score)
        top = jnp.max(score, axis=1, keepdims=True)
        top = (top + jnp.abs(top) * 0.0078125).astype(bf16).astype(f32)
        weight = jnp.where(live, jnp.exp(score - top), 0.0).astype(bf16)
        total = jnp.sum(weight.astype(f32), axis=1, keepdims=True)
        out = jnp.dot(weight, value_ref[p], preferred_element_type=f32)
        place = place_ref[p, 1]
        high = total.astype(bf16).astype(f32)
        note = jnp.where(kind == 0, top, jnp.where(kind == 1, high, total - high))
        entry_out[place] = out
        entry_note[place] = jnp.where(kind == 3, sent_id_ref[p : p + 1, :], note)
        local_out_ref[p] = out
        notes.append(jnp.where(kind == 3, local_id_ref[p : p + 1, :], note))
        if p % 4 == 3:
            a, b, c, d = notes[p - 3 : p + 1]
            local_note_ref[p // 4] = jnp.where(
                group == 0, a, jnp.where(group == 1, b, jnp.where(group == 2, c, d))
            )
    for jj in range(n_inst // 2):
        rows = []
        for j in (2 * jj, 2 * jj + 1):
            a, b, c, d = [entry_note[j * lent_slots + k] for k in range(lent_slots)]
            rows += [entry_out[j * lent_slots + k] for k in range(lent_slots)]
            rows.append(
                jnp.where(group == 0, a, jnp.where(group == 1, b, jnp.where(group == 2, c, d)))
            )
        sent_ref[pl.ds(80 * jj, 80), :] = jnp.concatenate(rows, axis=0).astype(bf16)


def merge_kernel(
    got_ref, local_out_ref, local_note_ref, query_ref, new_key_ref, new_value_ref, weight_ref,
    attended_ref, send_ref, attended_rows,
):
    heads = 8
    rows, head_dim = query_ref.shape
    requests = rows // heads
    scale = head_dim ** (-0.5)
    outs, notes = [], []
    for jj in range(got_ref.shape[0] // 80):
        block = got_ref[pl.ds(80 * jj, 80), :].astype(f32)
        for start in (0, 40):
            outs.append([block[start + 8 * k : start + 8 * k + 8] for k in range(lent_slots)])
            notes.append(block[start + 32 : start + 40])
    for g in range(local_note_ref.shape[0]):
        outs.append([local_out_ref[4 * g + k] for k in range(lent_slots)])
        notes.append(local_note_ref[g])
    while len(notes) % 16:
        outs.append([jnp.zeros((heads, head_dim), f32)] * lent_slots)
        notes.append(jnp.full((heads, head_dim), -1.0, f32))
    turned = jnp.concatenate(
        [jnp.concatenate(notes[g : g + 16], axis=0).T[:16] for g in range(0, len(notes), 16)], axis=1
    )
    entries = turned.shape[1]
    head_of = lax.broadcasted_iota(jnp.int32, (1, entries), 1) % heads
    row_id = lax.broadcasted_iota(jnp.int32, (rows, entries), 0).astype(f32)

    spread = (requests, heads, head_dim)
    new_key = jnp.broadcast_to(new_key_ref[...].astype(f32)[:, None, :], spread).reshape(rows, head_dim)
    new_value = jnp.broadcast_to(new_value_ref[...].astype(f32)[:, None, :], spread).reshape(rows, head_dim)
    own = jnp.sum(query_ref[...].astype(f32) * new_key, axis=1, keepdims=True) * scale

    tops = []
    for k in range(lent_slots):
        whose = turned[4 * k + 3 : 4 * k + 4] * heads + head_of.astype(f32)
        tops.append(jnp.where(row_id == whose, turned[4 * k : 4 * k + 1], masked_score))
    most = jnp.maximum(jnp.maximum(tops[0], tops[1]), jnp.maximum(tops[2], tops[3]))
    top = jnp.maximum(jnp.max(most, axis=1, keepdims=True), own)
    own_weight = jnp.exp(own - top).astype(bf16).astype(f32)
    total = 0.0
    value = own_weight * new_value
    for k in range(lent_slots):
        factor = jnp.exp(tops[k] - top).astype(bf16)
        sums = turned[4 * k + 1 : 4 * k + 2] + turned[4 * k + 2 : 4 * k + 3]
        total = total + factor.astype(f32) * sums
        part = jnp.concatenate([out[k] for out in outs], axis=0).astype(bf16)
        value = value + jnp.dot(factor, part, preferred_element_type=f32)
    total = jnp.sum(total, axis=1, keepdims=True) + own_weight
    attended_rows[...] = (value / total).reshape(spread)
    attended = jnp.concatenate([attended_rows[:, h, :] for h in range(heads)], axis=1).astype(bf16)
    attended_ref[...] = attended
    other = 1 - lax.axis_index("tp") % 2
    width = send_ref.shape[1] // 4
    for n in range(4):
        at = pl.ds(pl.multiple_of((2 * n + other) * width, width), width)
        send_ref[:, n * width : (n + 1) * width] = jnp.dot(
            attended, weight_ref[:, at], preferred_element_type=f32
        ).astype(bf16)


def project_kernel(attended_ref, weight_ref, keep_ref):
    mine = lax.axis_index("tp") % 2
    width = keep_ref.shape[1] // 4
    attended = attended_ref[...]
    for n in range(4):
        at = pl.ds(pl.multiple_of((2 * n + mine) * width, width), width)
        keep_ref[:, n * width : (n + 1) * width] = jnp.dot(
            attended, weight_ref[:, at], preferred_element_type=f32
        )


def split_kernel(keep_ref, got_ref, own_ref, *send_refs):
    chip = lax.axis_index("tp") // 2
    width = own_ref.shape[1]
    for k in range(4):
        at = pl.ds(pl.multiple_of(lax.rem(chip + k, 4) * width, width), width)
        total = keep_ref[:, at] + got_ref[:, at].astype(f32)
        if k == 0:
            own_ref[...] = total
        else:
            send_refs[k - 1][...] = total.astype(bf16)


def vmem(n):
    return [pl.BlockSpec(memory_space=pltpu.VMEM)] * n


def smem(n):
    return [pl.BlockSpec(memory_space=pltpu.SMEM)] * n


def body(
    query, new_key, new_value, key_cache, value_cache, out_weight, lengths, block_owner, block_index
):
    req_local, heads_dev, head_dim = query.shape
    slot_count, block_len, _, _ = key_cache.shape
    n_inst = lengths.shape[0] // req_local
    ring_z = n_inst // ring_y
    n_tp = lax.axis_size("tp")
    rows = req_local * heads_dev
    features = out_weight.shape[1]
    params = pltpu.CompilerParams(vmem_limit_bytes=24 * 1024 * 1024)
    shape = jax.ShapeDtypeStruct

    flat_query = query.reshape(rows, head_dim)
    copies = pl.pallas_call(
        copies_kernel,
        out_shape=shape((ring_z, rows, head_dim), bf16),
        in_specs=vmem(1),
        out_specs=vmem(1)[0],
        compiler_params=params,
        cost_estimate=pl.CostEstimate(flops=20_000_000_000, bytes_accessed=1_000_000, transcendentals=0),
        name="copies",
    )(flat_query)
    row = lax.all_to_all(copies, "z", 0, 0, tiled=True).reshape(ring_z * rows, head_dim)
    from_rows = {0: row}
    for k in (1, 3, 2):
        pairs = [(i, (i + k) % ring_y) for i in range(ring_y)]
        from_rows[k] = lax.ppermute(row, "y", pairs)
    plan = pl.pallas_call(
        plan_kernel,
        out_shape=(shape((slot_count, head_dim), jnp.int32),) * 2
        + (shape((slot_count, head_dim), f32),) * 2,
        in_specs=smem(3) + [pl.BlockSpec(memory_space=pl.ANY)],
        out_specs=tuple(vmem(4)),
        scratch_shapes=[pltpu.SMEM((n_inst,), jnp.int32)],
        compiler_params=params,
        cost_estimate=pl.CostEstimate(flops=2_000_000_000, bytes_accessed=100_000, transcendentals=0),
        name="plan",
    )(block_owner, block_index, lengths, row)
    keys = key_cache.reshape(slot_count, block_len, head_dim)
    values = value_cache.reshape(slot_count, block_len, head_dim)
    sent_rows = (lent_slots + 1) * heads_dev
    sent, local_out, local_note = pl.pallas_call(
        attend_kernel,
        out_shape=(
            shape((n_inst * sent_rows, head_dim), bf16),
            shape((slot_count, heads_dev, head_dim), f32),
            shape((slot_count // lent_slots, heads_dev, head_dim), f32),
        ),
        in_specs=vmem(10),
        out_specs=tuple(vmem(3)),
        scratch_shapes=[
            pltpu.VMEM((n_inst * lent_slots + 1, heads_dev, head_dim), f32),
            pltpu.VMEM((n_inst * lent_slots + 1, heads_dev, head_dim), f32),
        ],
        compiler_params=params,
        name="attend",
    )(*plan, *[from_rows[k] for k in (0, 2, 3, 1)], keys, values)
    got = lax.all_to_all(
        sent.reshape(n_inst, sent_rows, head_dim), inst, 0, 0, tiled=True
    ).reshape(n_inst * sent_rows, head_dim)
    attended, for_core = pl.pallas_call(
        merge_kernel,
        out_shape=(
            shape((req_local, heads_dev * head_dim), bf16),
            shape((req_local, features // 2), bf16),
        ),
        in_specs=vmem(7),
        out_specs=tuple(vmem(2)),
        scratch_shapes=[pltpu.VMEM((req_local, heads_dev, head_dim), f32)],
        compiler_params=params,
        name="merge",
    )(
        got, local_out, local_note, flat_query,
        new_key.reshape(req_local, head_dim), new_value.reshape(req_local, head_dim), out_weight,
    )
    from_core = lax.ppermute(for_core, "tp", [(i, i ^ 1) for i in range(n_tp)])
    keep = pl.pallas_call(
        project_kernel,
        out_shape=shape((req_local, features // 2), f32),
        in_specs=vmem(2),
        out_specs=vmem(1)[0],
        compiler_params=params,
        cost_estimate=pl.CostEstimate(flops=200_000_000, bytes_accessed=4_000_000, transcendentals=0),
        name="project",
    )(attended, out_weight)
    width = features // n_tp
    own, *parts = pl.pallas_call(
        split_kernel,
        out_shape=(shape((req_local, width), f32),) + (shape((req_local, width), bf16),) * 3,
        in_specs=vmem(2),
        out_specs=tuple(vmem(4)),
        compiler_params=params,
        name="split",
    )(keep, from_core)
    total = own
    for k in (1, 2, 3):
        pairs = [(i, (i + 2 * k) % n_tp) for i in range(n_tp)]
        total = total + lax.ppermute(parts[k - 1], "tp", pairs).astype(f32)
    return total.astype(bf16)


def solution(mesh):
    shape = (ring_y, mesh.shape["inst"] // ring_y, mesh.shape["tp"])
    mesh = Mesh(mesh.devices.reshape(shape), ("y", "z", "tp"))
    placed = (
        P(inst, "tp", None),
        P(inst, "tp", None),
        P(inst, "tp", None),
        P(inst, None, "tp", None),
        P(inst, None, "tp", None),
        P("tp", None),
        P(),
        P(inst),
        P(inst),
    )
    return jax.shard_map(
        body, mesh=mesh, in_specs=placed, out_specs=P(inst, "tp"), check_vma=False
    )
```
